256 devices in a mesh: row: 16 (over z_hi, x, core), col: 16 (over y, z_lo).
Axes of the slice: x: 4, y: 4, z: 8 (z_hi: 2, z_lo: 4; z = z_hi * 4 + z_lo), core: 2. Of those that a mesh axis runs over, the one named last changes fastest.
Arguments:
- features: bfloat16 [131072, 128], P(('col', 'row')), may hold values from -240 to 240
- weight: bfloat16 [128, 256], replicated, may hold values from -0.5 to 0.5
- row_degree: int32 [131072], P(('row', 'col')), may hold values from 320 to 640
- col_degree: int32 [131072], P(('col', 'row')), may hold values from 320 to 640
- tile_cols: int32 [1024, 16, 6], P('row', 'col'), may hold values from 0 to 63, all different within a row
- slot_mask: int32 [1024, 16, 6], P('row', 'col'), may hold values 0 or 1
- tile_entries: bfloat16 [1024, 16, 6, 128, 128], P('row', 'col'), may hold values from 0 to 1, as said below
- cotangent: bfloat16 [131072, 256], P(('row', 'col')), may hold values from -192 to 192
Outputs:
- hidden: bfloat16 [131072, 256], P(('row', 'col'))
- weight_grad: float32 [128, 256], replicated
- feature_grad: bfloat16 [131072, 128], P(('col', 'row'))
The draws below stay inside these ranges and needn't reach their ends.
Inputs may be any that keep to these rules, and one draw needn't show every extreme that they name: `tile_cols`: the 6 slots of each tile row and column block name different column tiles. `tile_entries`: every entry is 0 or 1.
All inputs are finite; a program needn't handle non-finite values. No bound on the sum of `slot_mask` on one device may be relied on, other than what follows from the above.
Results may differ from the reference program's by a relative error of at most 0.03.
Values may be sent and summed in bfloat16 or wider, within the bound.
A program may use at most 128 MiB of HBM per device.

```python
import math
import jax
import jax.numpy as jnp
from jax import lax

F = 128
H = 256
TILE = 128
K = 6
NODES = 131072
N_ROW = 16
N_COL = 16


def draw_tile_entries(key, part):
    key = jax.random.fold_in(key, 7)
    share = min(0.5, 96.0 / (N_COL * K * TILE * 0.875))
    uniform_draw = jax.random.uniform(key, (NODES // TILE, N_COL, K, TILE, TILE), jnp.float32)
    return jnp.where(uniform_draw < share, 1.0, 0.0).astype(jnp.bfloat16)


def touch_ends(result, stream_key, low, top_value):
    longest = result.shape.index(max(result.shape))
    spots = []
    for shift in (0, 1):
        where = [jax.random.randint(jax.random.fold_in(stream_key, axis), (), 0, length) for axis, length in enumerate(result.shape)]
        where[longest] = (where[longest] + shift) % result.shape[longest]
        spots.append(tuple(where))
    return result.at[spots[0]].set(low).at[spots[1]].set(top_value)


def block_levels(own_key, shape, split, low, largest):
    loudness = 1.0
    for position, blocks in split:
        draws = jax.random.uniform(jax.random.fold_in(jax.random.fold_in(own_key, 6), position), (blocks,), jnp.float32, low / len(split), largest / len(split))
        loudness = loudness * jnp.repeat(jnp.exp(draws), shape[position] // blocks).reshape((-1,) + (1,) * (len(shape) - 1 - position))
    return loudness


def choose_distinct(rng, rows, count, top, lift):
    ranking = jax.random.permutation(jax.random.fold_in(rng, 1), count)
    favour = ranking
    for power in range(3):
        favour = favour * favour // count
    favour = favour * lift // count
    chance = jax.random.randint(jax.random.fold_in(rng, 2), (rows, count), 0, 4096) + favour
    sure = jax.random.permutation(jax.random.fold_in(rng, 3), rows)[jnp.arange(count) % rows]
    chance = jnp.where(jnp.arange(rows)[:, None] == sure[None, :], 1 << 14, chance)
    merit = chance * count + jnp.arange(count)
    return lax.top_k(merit.astype(jnp.int32), top)[1].astype(jnp.int32)


def scatter_about(own_key, dims, spread, reach, cuts=(), kind=jnp.bfloat16):
    drawn = jax.random.normal(own_key, dims, jnp.float32) * spread
    if len(cuts) > 0:
        drawn = block_levels(own_key, dims, cuts, -0.22, 0.18) * drawn
    return jnp.clip(drawn, min=-reach, max=reach).astype(kind)


def setup_inputs(seed: int = 0) -> dict:
    seeds = jax.random.split(jax.random.key(seed), 9)
    features = scatter_about(seeds[0], (NODES, F), 40.0, 240.0, ((0, 256),))
    weight = scatter_about(seeds[1], (F, H), F ** -0.5, 0.5)
    row_degree = touch_ends(jax.random.randint(seeds[2], (NODES,), 320, 641), jax.random.fold_in(seeds[2], 1), 320, 640).astype(jnp.int32)
    col_degree = touch_ends(jax.random.randint(seeds[3], (NODES,), 320, 641), jax.random.fold_in(seeds[3], 1), 320, 640).astype(jnp.int32)
    tile_cols = choose_distinct(seeds[4], (NODES // TILE) * N_COL, NODES // (TILE * N_COL), K, 768).reshape((NODES // TILE, N_COL, K))
    slot_mask = touch_ends((jax.random.randint(seeds[5], (NODES // TILE, N_COL, K), 0, 8) < 7).astype(jnp.int32), jax.random.fold_in(seeds[5], 1), 0, 1)
    tile_entries = draw_tile_entries(jax.random.fold_in(seeds[8], 71), 0)
    cotangent = scatter_about(seeds[7], (NODES, H), 32.0, 192.0, ((0, 256),))
    return dict(features=features, weight=weight, row_degree=row_degree, col_degree=col_degree, tile_cols=tile_cols, slot_mask=slot_mask, tile_entries=tile_entries, cotangent=cotangent)


def reference(features, weight, row_degree, col_degree, tile_cols, slot_mask, tile_entries, cotangent):
    col_scale = lax.rsqrt(col_degree.astype(jnp.float32))
    row_scale = lax.rsqrt(row_degree.astype(jnp.float32))
    scaled = (features.astype(jnp.float32) * col_scale[:, None]).astype(jnp.bfloat16)
    scaled_tiles = scaled.reshape(NODES // TILE, TILE, F)
    per_block = NODES // (N_COL * TILE)
    offsets = (jnp.arange(N_COL, dtype=jnp.int32) * per_block).astype(jnp.int32)
    global_cols = (tile_cols + offsets[None, :, None]).astype(jnp.int32)
    live_slots = slot_mask.astype(jnp.float32)

    def forward_row(carried, inputs):
        index_row, live_row, entry_row = inputs
        gathered = scaled_tiles[index_row].astype(jnp.float32) * live_row[:, :, None, None]
        partial_blocks = jnp.einsum('jkab,jkbf->jaf', entry_row.astype(jnp.float32), gathered)
        rounded = lax.optimization_barrier(partial_blocks.astype(jnp.bfloat16))
        summed = lax.optimization_barrier(jnp.sum(rounded.astype(jnp.float32), axis=0))
        return (carried, summed)
    _, aggregate = lax.scan(forward_row, jnp.zeros((), jnp.float32), (global_cols, live_slots, tile_entries))
    aggregate = aggregate.reshape(NODES, F)
    smoothed = (aggregate * row_scale[:, None]).astype(jnp.bfloat16)
    pre_act = jnp.dot(smoothed, weight, preferred_element_type=jnp.float32)
    hidden = jax.nn.gelu(pre_act).astype(jnp.bfloat16)
    _, pull_back = jax.vjp(jax.nn.gelu, pre_act)
    grad_pre = pull_back(cotangent.astype(jnp.float32))[0].astype(jnp.bfloat16)
    weight_grad = jnp.dot(smoothed.T, grad_pre, preferred_element_type=jnp.float32) * (1.0 / (32.0 * math.sqrt(NODES)))
    grad_smooth = (jnp.dot(grad_pre, weight.T, preferred_element_type=jnp.float32) * row_scale[:, None]).astype(jnp.bfloat16)
    grad_tiles = grad_smooth.reshape(NODES // TILE, TILE, F)
    block_rows = NODES // TILE // N_ROW

    def regroup(array):
        return array.reshape((N_ROW, block_rows) + array.shape[1:])

    def backward_row(summed, inputs):
        index_row, live_row, entry_row, grad_row = inputs
        contrib = jnp.einsum('jkab,af->jkbf', entry_row.astype(jnp.float32), grad_row.astype(jnp.float32))
        contrib = contrib * live_row[:, :, None, None]
        summed = summed.at[index_row.reshape(-1)].add(contrib.reshape(-1, TILE, F))
        return (summed, None)

    def backward_block(total, inputs):
        partial_sum, _ = lax.scan(backward_row, jnp.zeros((NODES // TILE, TILE, F), jnp.float32), inputs)
        rounded = lax.optimization_barrier(partial_sum.astype(jnp.bfloat16))
        return (total + rounded.astype(jnp.float32), None)
    column_total, _ = lax.scan(backward_block, jnp.zeros((NODES // TILE, TILE, F), jnp.float32), (regroup(global_cols), regroup(live_slots), regroup(tile_entries), regroup(grad_tiles)))
    feature_grad = (column_total.reshape(NODES, F) * col_scale[:, None]).astype(jnp.bfloat16)
    return (hidden, weight_grad, feature_grad)
```

```python
import functools
import math

import jax
import jax.numpy as jnp
from jax import lax
from jax.experimental import pallas as pl
from jax.experimental.pallas import tpu as pltpu
from jax.sharding import PartitionSpec as P

MESH = pl.DeviceIdType.MESH
BF = jnp.bfloat16
F32 = jnp.float32

T = 128
B = 4
K = 6
TILES = 64
SLOTS = TILES * K
EMPTY = SLOTS
ZERO = TILES
FWD_ORDER = (2, 1, 3, 0)
BWD_ORDER = (0, 1, 3, 2)
N_COPIES = 160


def coords():
    row, col = lax.axis_index("row"), lax.axis_index("col")
    return row // 8, lax.rem(row // 2, 4), lax.rem(row, 2), col // 4, lax.rem(col, 4)


def mod4(value):
    return lax.rem(value + 8, 4)


class Copies:
    def __init__(self, send_sems, recv_sems):
        self.sems = (send_sems, recv_sems)
        self.made = []
        self.place = coords()

    def device(self, x=0, y=0, z=0, core=0, half=0):
        mz, mx, mc, my, ml = self.place
        row = lax.rem(mz + half, 2) * 8 + mod4(mx + x) * 2 + lax.rem(mc + core, 2)
        return (row, mod4(my + y) * 4 + mod4(ml + z))

    def send(self, src, dst, **shift):
        n = len(self.made)
        copy = pltpu.make_async_remote_copy(
            src_ref=src,
            dst_ref=dst,
            send_sem=self.sems[0].at[n],
            recv_sem=self.sems[1].at[n],
            device_id=self.device(**shift),
            device_id_type=MESH,
        )
        copy.start()
        self.made.append(copy)
        return copy


PEERS = (
    [dict(x=1), dict(x=3), dict(x=2)]
    + [dict(y=1), dict(y=3), dict(y=2)]
    + [dict(z=1), dict(z=3), dict(z=2)]
    + [dict(core=1), dict(half=1)]
)


def blocks(ref, first, count):
    return ref.at[pl.ds(first, count)]


def kernel(
    grad_scale,
    index_ref, prev_ref, last_ref, entries_hbm, feat_ref, weight_ref, rowdeg_ref, coldeg_ref, cot_ref,
    hidden_ref, wgrad_ref, fgrad_ref,
    entries, panel, parts, up1, down1, up2, down2, zsend, zrecv, total,
    gpanel, chain, wlocal, wy, wz, wx, wc, wh, wfull,
    csend, crecv, xsum, xup1, xdown1, xup2, xdown2, hsend, hrecv,
    load_sems, send_sems, recv_sems,
):
    net = Copies(send_sems, recv_sems)
    mz, mx, mc, my, ml = net.place
    row, col = lax.axis_index("row"), lax.axis_index("col")

    n_loads = 8
    share = TILES // n_loads
    loads = []
    for n in range(n_loads):
        load = pltpu.make_async_copy(
            entries_hbm.at[pl.ds(n * share, share)], entries.at[pl.ds(n * share, share)], load_sems.at[n]
        )
        load.start()
        loads.append(load)

    barrier = pltpu.get_barrier_semaphore()
    for shift in PEERS:
        pl.semaphore_signal(barrier, inc=1, device_id=net.device(**shift), device_id_type=MESH)

    col_scale = lax.rsqrt(coldeg_ref[...].astype(F32))
    row_scale = lax.rsqrt(rowdeg_ref[...].astype(F32))

    def down_rows(scale, t):
        return jnp.broadcast_to(scale[t : t + 1, :], (T, T)).T

    mine = row * B
    for t in range(B):
        panel[mine + t] = (feat_ref[pl.ds(t * T, T), :].astype(F32) * down_rows(col_scale, t)).astype(BF)
    panel[ZERO] = jnp.zeros((T, T), BF)
    chain[EMPTY] = jnp.zeros((T, T), F32)
    pl.semaphore_wait(barrier, len(PEERS))

    def panel_at(half, x, first=0, count=B):
        place = lax.rem(mz + half, 2) * 8 + mod4(mx + x) * 2 + mc
        return blocks(panel, place * B + first, count)

    def pass_on(part, dx, first, count, **shift):
        ref = panel_at(part, dx, first, count)
        return net.send(ref, ref, **shift)

    from_core = []

    def share_core(half, x, first=0, count=B):
        from_core.append(pass_on(half, x, first, count, core=1))

    over = [pass_on(0, 0, t, 1, half=1) for t in range(B)]
    right = pass_on(0, 0, 0, B, x=1)
    left = pass_on(0, 0, 0, B, x=3)
    share_core(0, 0)
    right.wait_recv()
    fright = pass_on(0, -1, 0, 2, x=1)
    left.wait_recv()
    fleft = pass_on(0, 1, 2, 2, x=3)
    share_core(0, -1)
    share_core(0, 1)
    rights, lefts = [], []
    for t in range(B):
        over[t].wait_recv()
        rights.append(pass_on(1, 0, t, 1, x=1))
        lefts.append(pass_on(1, 0, t, 1, x=3))
    share_core(1, 0)
    fright.wait_recv()
    fleft.wait_recv()
    share_core(0, 2)
    frights, flefts = [], []
    for t in range(B):
        rights[t].wait_recv()
        if t < 2:
            frights.append(pass_on(1, -1, t, 1, x=1))
        lefts[t].wait_recv()
        if t >= 2:
            flefts.append(pass_on(1, 1, t, 1, x=3))
    share_core(1, -1)
    share_core(1, 1)
    for copy in frights + flefts:
        copy.wait_recv()
    share_core(1, 2)
    for load in loads:
        load.wait()
    for copy in from_core:
        copy.wait_recv()

    def product(y, z):
        first = (mod4(my + y) * 4 + mod4(ml + z)) * B

        def tile(t, carry):
            r = first + t
            acc = jnp.zeros((T, T), F32)
            for k in range(0, K, 2):
                lhs = jnp.concatenate([entries[r, k], entries[r, k + 1]], axis=1)
                rhs = jnp.concatenate(
                    [panel[index_ref[r * K + k]], panel[index_ref[r * K + k + 1]]], axis=0
                )
                acc = acc + jnp.dot(lhs, rhs, preferred_element_type=F32)
            parts[r] = acc.astype(BF)
            return carry

        lax.fori_loop(0, B, tile, 0)
        return first

    def add_to(ref, first, count, other):
        where = pl.ds(first, count)
        ref[where] = (ref[where].astype(F32) + other.astype(F32)).astype(BF)

    ups1, downs1, ups2, downs2, zs = [], [], [], [], []
    for q in range(4):
        first = product(2, FWD_ORDER[q])
        ups1.append(net.send(blocks(parts, first, 2), up1.at[q], y=1))
        downs1.append(net.send(blocks(parts, first + 2, 2), down1.at[q], y=3))
    for q in range(4):
        first = product(1, FWD_ORDER[q])
        ups1[q].wait_recv()
        add_to(parts, first, 2, up1[q])
        ups2.append(net.send(blocks(parts, first, B), up2.at[q], y=1))
        first = product(3, FWD_ORDER[q])
        downs1[q].wait_recv()
        add_to(parts, first + 2, 2, down1[q])
        downs2.append(net.send(blocks(parts, first, B), down2.at[q], y=3))
    firsts = [product(0, FWD_ORDER[q]) for q in range(4)]
    for q in range(4):
        ups2[q].wait_recv()
        downs2[q].wait_recv()
        here = parts[pl.ds(firsts[q], B)].astype(F32) + up2[q].astype(F32) + down2[q].astype(F32)
        if q < 3:
            zsend[q] = here.astype(BF)
            zs.append(net.send(zsend.at[q], zrecv.at[q], z=FWD_ORDER[q]))
        else:
            total[...] = here
    for copy in zs:
        copy.wait_recv()

    weight = weight_ref[...]
    lean = math.sqrt(2.0 / math.pi)
    for t in range(B):
        rows = pl.ds(t * T, T)
        aggregate = total[t]
        for q in range(3):
            aggregate = aggregate + zrecv[q, t].astype(F32)
        smoothed = (aggregate * down_rows(row_scale, t)).astype(BF)
        pre = jnp.dot(smoothed, weight, preferred_element_type=F32)
        square = pre * pre
        slope = jnp.tanh(lean * pre * (1.0 + 0.044715 * square))
        gate = 0.5 * (1.0 + slope)
        hidden_ref[rows, :] = (pre * gate).astype(BF)
        steep = gate + 0.5 * pre * (1.0 - slope * slope) * (lean * (1.0 + 3.0 * 0.044715 * square))
        grad_pre = (cot_ref[rows, :].astype(F32) * steep).astype(BF)
        spread = lax.dot_general(weight, grad_pre, (((1,), (1,)), ((), ())), preferred_element_type=F32)
        gpanel[col * B + t] = (spread * row_scale[t : t + 1, :]).astype(BF)
        outer = lax.dot_general(smoothed, grad_pre, (((0,), (0,)), ((), ())), preferred_element_type=F32)
        if t == 0:
            wlocal[...] = outer
        else:
            wlocal[...] += outer

    def grads_at(y, z, first=0, count=B):
        place = mod4(my + y) * 4 + mod4(ml + z)
        return blocks(gpanel, place * B + first, count)

    def hand_on(dy, dz, first, count, **shift):
        ref = grads_at(dy, dz, first, count)
        return net.send(ref, ref, **shift)

    def back(y, z):
        first = (mod4(my + y) * 4 + mod4(ml + z)) * B

        def tile(t, carry):
            r = first + t
            grads = gpanel[r]
            for k in range(0, K, 2):
                slot = r * K + k
                rhs = jnp.concatenate([entries[r, k], entries[r, k + 1]], axis=1)
                both = jnp.dot(grads, rhs, preferred_element_type=F32)
                one = chain[prev_ref[slot]] + both[:, :T]
                two = chain[prev_ref[slot + 1]] + both[:, T:]
                chain[slot] = one
                chain[slot + 1] = two
            return carry

        lax.fori_loop(0, B, tile, 0)

    gups, gdowns, fups, fdowns = [], [], [], []
    gups.append(hand_on(0, 0, 0, B, y=1))
    gdowns.append(hand_on(0, 0, 0, B, y=3))
    gz = [None] + [hand_on(0, 0, 0, B, z=-BWD_ORDER[q]) for q in (1, 2, 3)]
    wys = [
        net.send(wlocal.at[pl.ds(mod4(my + d) * 32, 32)], wy.at[d - 1], y=d) for d in (1, 2, 3)
    ]
    back(0, 0)
    for q in range(4):
        off = BWD_ORDER[q]
        if q < 3:
            nxt = BWD_ORDER[q + 1]
        gups[q].wait_recv()
        fups.append(hand_on(-1, off, 0, 2, y=1))
        gdowns[q].wait_recv()
        fdowns.append(hand_on(1, off, 2, 2, y=3))
        if q < 3:
            gz[q + 1].wait_recv()
            gups.append(hand_on(0, nxt, 0, B, y=1))
            gdowns.append(hand_on(0, nxt, 0, B, y=3))
        back(-1, off)
        back(1, off)
        if q < 3:
            back(0, nxt)
        if q == 0:
            for copy in wys:
                copy.wait_recv()
            wz[3] = wlocal[pl.ds(my * 32, 32), :] + wy[0] + wy[1] + wy[2]
            wzs = [
                net.send(wz.at[3, pl.ds(mod4(ml + d) * 8, 8)], wz.at[d - 1, pl.ds(0, 8)], z=d) for d in (1, 2, 3)
            ]
        if q == 1:
            for copy in wzs:
                copy.wait_recv()
            wx[mx] = wz[3, pl.ds(ml * 8, 8), :] + wz[0, :8, :] + wz[1, :8, :] + wz[2, :8, :]
            wxs = [net.send(wx.at[mx], wx.at[mx], x=d) for d in (1, 2, 3)]
        if q == 2:
            for copy in wxs:
                copy.wait_recv()
            wc[0] = wx[0] + wx[1] + wx[2] + wx[3]
            wcs = net.send(wc.at[0], wc.at[1], core=1)
        if q == 3:
            wcs.wait_recv()
            wh[0] = wc[0] + wc[1]
            whs = net.send(wh.at[0], wh.at[1], half=1)
        fups[q].wait_recv()
        fdowns[q].wait_recv()
        back(2, off)

    def column(half, x, core):
        return (lax.rem(mz + half, 2) * 8 + mod4(mx + x) * 2 + lax.rem(mc + core, 2)) * B

    order = [(half, x) for half in (1, 0) for x in (2, 1, 3, 0)]
    cores = []
    for n, (half, x) in enumerate(order):
        first = column(half, x, 1)
        for t in range(B):
            csend[n, t] = chain[last_ref[first + t]].astype(BF)
        cores.append(net.send(csend.at[n], crecv.at[n], core=1))
    xups1, xdowns1, xups2, xdowns2 = [], [], [], []

    def chip_sum(n):
        half, x = order[n]
        first = column(half, x, 0)
        cores[n].wait_recv()
        for t in range(B):
            xsum[n, t] = (chain[last_ref[first + t]] + crecv[n, t].astype(F32)).astype(BF)

    for h in range(2):
        chip_sum(4 * h)
        xups1.append(net.send(xsum.at[4 * h, pl.ds(0, 2)], xup1.at[h], x=1))
        xdowns1.append(net.send(xsum.at[4 * h, pl.ds(2, 2)], xdown1.at[h], x=3))
    for h in range(2):
        chip_sum(4 * h + 1)
        chip_sum(4 * h + 2)
        xups1[h].wait_recv()
        xsum[4 * h + 1, :2] = (xsum[4 * h + 1, :2].astype(F32) + xup1[h].astype(F32)).astype(BF)
        xups2.append(net.send(xsum.at[4 * h + 1], xup2.at[h], x=1))
        xdowns1[h].wait_recv()
        xsum[4 * h + 2, 2:] = (xsum[4 * h + 2, 2:].astype(F32) + xdown1[h].astype(F32)).astype(BF)
        xdowns2.append(net.send(xsum.at[4 * h + 2], xdown2.at[h], x=3))
        chip_sum(4 * h + 3)

    whs.wait_recv()
    wrows = my * 32 + ml * 8
    wfull[pl.ds(wrows, 8), :] = (wh[0] + wh[1]) * grad_scale
    wzs2 = [
        net.send(wfull.at[pl.ds(wrows, 8)], wfull.at[pl.ds(wrows, 8)], z=d) for d in (1, 2, 3)
    ]

    xups2[0].wait_recv()
    xdowns2[0].wait_recv()
    hsend[...] = (xsum[3].astype(F32) + xup2[0].astype(F32) + xdown2[0].astype(F32)).astype(BF)
    across = net.send(hsend, hrecv, half=1)
    for copy in wzs2:
        copy.wait_recv()
    wband = wfull.at[pl.ds(my * 32, 32)]
    wys2 = [net.send(wband, wband, y=d) for d in (1, 2, 3)]
    xups2[1].wait_recv()
    xdowns2[1].wait_recv()
    across.wait_recv()
    for t in range(B):
        tile = xsum[7, t].astype(F32) + xup2[1, t].astype(F32) + xdown2[1, t].astype(F32) + hrecv[t].astype(F32)
        fgrad_ref[pl.ds(t * T, T), :] = (tile * col_scale[t : t + 1, :]).T.astype(BF)
    for copy in wys2:
        copy.wait_recv()
    wgrad_ref[...] = wfull[...]
    for copy in net.made:
        copy.wait_send()


def chains(tile_cols, slot_mask):
    index = jnp.where(slot_mask[:, 0, :] > 0, tile_cols[:, 0, :], ZERO).reshape(SLOTS)
    col = lax.axis_index("col")
    my, ml = col // 4, lax.rem(col, 4)
    slot = jnp.arange(SLOTS, dtype=jnp.int32)
    r = slot // K
    dy = lax.rem(r // 16 - my + 4, 4)
    dz = lax.rem(lax.rem(r // 4, 4) - ml + 4, 4)
    turns = [(0, 0)]
    for q in range(4):
        turns += [(3, BWD_ORDER[q]), (1, BWD_ORDER[q])]
        if q < 3:
            turns.append((0, BWD_ORDER[q + 1]))
        turns.append((2, BWD_ORDER[q]))
    turn = jnp.zeros((SLOTS,), jnp.int32)
    for n, (y, z) in enumerate(turns):
        turn = jnp.where((dy == y) & (dz == z), n, turn)
    key = (turn * (B * K) + lax.rem(slot, B * K)) * 512 + slot
    same = (index[:, None] == index[None, :]) & (key[None, :] < key[:, None])
    prev = jnp.max(jnp.where(same, key[None, :], -1), axis=1)
    prev = jnp.where((prev >= 0) & (index < ZERO), lax.rem(prev, 512), EMPTY)
    tiles = jnp.arange(TILES, dtype=jnp.int32)
    last = jnp.max(jnp.where(index[None, :] == tiles[:, None], key[None, :], -1), axis=1)
    last = jnp.where(last >= 0, lax.rem(last, 512), EMPTY)
    return index, prev, last


def body(features, weight, row_degree, col_degree, tile_cols, slot_mask, tile_entries, cotangent):
    index, prev, last = chains(tile_cols, slot_mask)
    vmem = pl.BlockSpec(memory_space=pltpu.VMEM)
    smem = pl.BlockSpec(memory_space=pltpu.SMEM)
    nodes, hidden_width = cotangent.shape
    count = nodes * lax.axis_size("row") * lax.axis_size("col")
    grad_scale = 1.0 / (32.0 * math.sqrt(count))

    def tiles(*lead, dtype=BF):
        return pltpu.VMEM((*lead, T, T), dtype)

    def wide(*shape):
        return pltpu.VMEM((*shape, hidden_width), F32)

    return pl.pallas_call(
        functools.partial(kernel, grad_scale),
        out_shape=(
            jax.ShapeDtypeStruct((nodes, hidden_width), BF),
            jax.ShapeDtypeStruct((T, hidden_width), F32),
            jax.ShapeDtypeStruct((nodes, T), BF),
        ),
        in_specs=[smem] * 3 + [pl.BlockSpec(memory_space=pl.ANY)] + [vmem] * 5,
        out_specs=(vmem, vmem, vmem),
        scratch_shapes=[
            tiles(TILES, K), tiles(TILES + 1), tiles(TILES),
            tiles(4, 2), tiles(4, 2), tiles(4, B), tiles(4, B), tiles(3, B), tiles(3, B), tiles(B, dtype=F32),
            tiles(TILES), tiles(SLOTS + 1, dtype=F32),
            wide(T), wide(3, 32), wide(4, 32), wide(4, 8), wide(2, 8), wide(2, 8), wide(T),
            tiles(8, B), tiles(8, B), tiles(8, B),
            tiles(2, 2), tiles(2, 2), tiles(2, B), tiles(2, B), tiles(B), tiles(B),
            pltpu.SemaphoreType.DMA((8,)),
            pltpu.SemaphoreType.DMA((N_COPIES,)),
            pltpu.SemaphoreType.DMA((N_COPIES,)),
        ],
        compiler_params=pltpu.CompilerParams(
            collective_id=0, has_side_effects=True, vmem_limit_bytes=60 * 1024 * 1024
        ),
        name="graph_layer",
    )(
        index, prev, last, tile_entries.reshape(TILES, K, T, T), features, weight,
        row_degree.reshape(B, T), col_degree.reshape(B, T), cotangent,
    )


def solution(mesh):
    return jax.shard_map(
        body,
        mesh=mesh,
        in_specs=(
            P(("col", "row"), None),
            P(),
            P(("row", "col")),
            P(("col", "row")),
            P("row", "col", None),
            P("row", "col", None),
            P("row", "col", None, None, None),
            P(("row", "col"), None),
        ),
        out_specs=(P(("row", "col"), None), P(), P(("col", "row"), None)),
        check_vma=False,
    )
```

```python
import functools
import math

import jax
import jax.numpy as jnp
from jax import lax
from jax.experimental import pallas as pl
from jax.experimental.pallas import tpu as pltpu
from jax.sharding import PartitionSpec as P

MESH = pl.DeviceIdType.MESH
BF = jnp.bfloat16
F32 = jnp.float32

T = 128
B = 4
K = 6
TILES = 64
SLOTS = TILES * K
EMPTY = SLOTS
ZERO = TILES
FWD_ORDER = (3, 2, 1, 0)
TURNS = ((0, 0), (0, 1), (3, 0), (1, 0), (0, 2), (0, 3), (3, 1), (1, 1), (3, 2), (1, 2), (3, 3), (1, 3))
TURNS += ((2, 0), (2, 1), (2, 2), (2, 3))
N_COPIES = 160
N_LOADS = 8
LAST = 6
INDEX = 8


def coords():
    row, col = lax.axis_index("row"), lax.axis_index("col")
    return row // 8, lax.rem(row // 2, 4), lax.rem(row, 2), col // 4, lax.rem(col, 4)


def mod4(value):
    return lax.rem(value + 8, 4)


def masked(z, mask):
    return (z, z + 1 - 2 * lax.rem(z, 2), mod4(z + 2), 3 - z)[mask]


class Copies:
    def __init__(self, send_sems, recv_sems):
        self.sems = (send_sems, recv_sems)
        self.made = []
        self.place = coords()

    def device(self, x=0, y=0, z=0, core=0, half=0):
        mz, mx, mc, my, ml = self.place
        row = lax.rem(mz + half, 2) * 8 + mod4(mx + x) * 2 + lax.rem(mc + core, 2)
        return (row, mod4(my + y) * 4 + masked(ml, z))

    def send(self, src, dst, **shift):
        n = len(self.made)
        copy = pltpu.make_async_remote_copy(
            src_ref=src,
            dst_ref=dst,
            send_sem=self.sems[0].at[n],
            recv_sem=self.sems[1].at[n],
            device_id=self.device(**shift),
            device_id_type=MESH,
        )
        copy.start()
        self.made.append(copy)
        return copy


PEERS = (
    [dict(x=1), dict(x=3), dict(x=2)]
    + [dict(y=1), dict(y=3), dict(y=2)]
    + [dict(z=1), dict(z=3), dict(z=2)]
    + [dict(core=1), dict(half=1)]
)


def blocks(ref, first, count):
    return ref.at[pl.ds(first, count)]


def kernel(
    grad_scale,
    cols_hbm, mask_hbm, entries_hbm, feat_hbm, weight_hbm, rowdeg_hbm, coldeg_hbm, cot_hbm,
    hidden_hbm, wgrad_hbm, fgrad_hbm,
    cols_ref, mask_ref, feat_ref, weight_ref, rowdeg_ref, coldeg_ref, cot_ref, hidden_ref, fgrad_ref, found, places,
    entries, panel, parts, up1, down1, up2, down2, zsend, zrecv, total,
    gpanel, chain, wlocal, wy, wz, wx, wc, wh, wfull,
    csend, crecv, xsum, xup1, xdown1, xup2, xdown2, hsend, hrecv,
    load_sems, io_sems, send_sems, recv_sems,
):
    net = Copies(send_sems, recv_sems)
    mz, mx, mc, my, ml = net.place
    row, col = lax.axis_index("row"), lax.axis_index("col")

    barrier = pltpu.get_barrier_semaphore()
    for shift in PEERS:
        pl.semaphore_signal(barrier, inc=1, device_id=net.device(**shift), device_id_type=MESH)

    moves = []

    def move(src, dst):
        copy = pltpu.make_async_copy(src, dst, io_sems.at[len(moves)])
        copy.start()
        moves.append(copy)
        return copy

    got_coldeg = move(coldeg_hbm, coldeg_ref)
    got_feat = move(feat_hbm, feat_ref)
    got_cols = move(cols_hbm, cols_ref)
    got_mask = move(mask_hbm, mask_ref)
    got_rowdeg = move(rowdeg_hbm, rowdeg_ref)
    got_weight = move(weight_hbm, weight_ref)
    got_cot = move(cot_hbm, cot_ref)
    share = TILES // N_LOADS
    loads = []
    for n in range(N_LOADS):
        load = pltpu.make_async_copy(
            entries_hbm.at[pl.ds(n * share, share)], entries.at[pl.ds(n * share, share)], load_sems.at[n]
        )
        load.start()
        loads.append(load)

    got_coldeg.wait()
    got_feat.wait()
    col_scale = lax.rsqrt(coldeg_ref[...].astype(F32))

    def down_rows(scale, t):
        return jnp.broadcast_to(scale[t : t + 1, :], (T, T)).T

    mine = row * B
    for t in range(B):
        panel[mine + t] = (feat_ref[pl.ds(t * T, T), :].astype(F32) * down_rows(col_scale, t)).astype(BF)
    panel[ZERO] = jnp.zeros((T, T), BF)
    chain[EMPTY] = jnp.zeros((T, T), F32)
    pl.semaphore_wait(barrier, len(PEERS))

    def panel_at(half, x, first=0, count=B):
        place = lax.rem(mz + half, 2) * 8 + mod4(mx + x) * 2 + mc
        return blocks(panel, place * B + first, count)

    def pass_on(part, dx, first, count, **shift):
        ref = panel_at(part, dx, first, count)
        return net.send(ref, ref, **shift)

    from_core = []

    def share_core(half, x, first=0, count=B):
        from_core.append(pass_on(half, x, first, count, core=1))

    halves = (0, 2)
    over = [pass_on(0, 0, t, 2, half=1) for t in halves]
    right = pass_on(0, 0, 0, B, x=1)
    left = pass_on(0, 0, 0, B, x=3)
    share_core(0, 0)

    got_cols.wait()
    got_mask.wait()
    find_places(cols_ref, mask_ref, found, my, ml)
    got_places = move(found, places)

    right.wait_recv()
    fright = pass_on(0, -1, 0, 2, x=1)
    left.wait_recv()
    fleft = pass_on(0, 1, 2, 2, x=3)
    share_core(0, -1)
    share_core(0, 1)
    others = []
    for t, copy in zip(halves, over):
        copy.wait_recv()
        others.append([pass_on(1, 0, t, 2, x=d) for d in (1, 3, 2)])
        share_core(1, 0, t, 2)
    fright.wait_recv()
    fleft.wait_recv()
    share_core(0, 2)
    for t, copies in zip(halves, others):
        for copy, d in zip(copies, (-1, 1, 2)):
            copy.wait_recv()
            share_core(1, d, t, 2)
    for load in loads:
        load.wait()
    for copy in from_core:
        copy.wait_recv()
    got_places.wait()

    def product(y, z):
        first = (mod4(my + y) * 4 + masked(ml, z)) * B

        def tile(r):
            acc = jnp.zeros((T, T), F32)
            for k in range(0, K, 2):
                lhs = jnp.concatenate([entries[r, k], entries[r, k + 1]], axis=1)
                rhs = jnp.concatenate(
                    [panel[places[INDEX + k, r]], panel[places[INDEX + k + 1, r]]], axis=0
                )
                acc = acc + jnp.dot(lhs, rhs, preferred_element_type=F32)
            parts[r] = acc.astype(BF)

        for t in range(B):
            tile(first + t)
        return first

    def add_to(ref, first, count, other):
        where = pl.ds(first, count)
        ref[where] = (ref[where].astype(F32) + other.astype(F32)).astype(BF)

    ups1, downs1, ups2, downs2, zs = [], [], [], [], []
    for q in range(4):
        first = product(2, FWD_ORDER[q])
        ups1.append(net.send(blocks(parts, first, 2), up1.at[q], y=1))
        downs1.append(net.send(blocks(parts, first + 2, 2), down1.at[q], y=3))
    def second(q):
        first = product(1, FWD_ORDER[q])
        ups1[q].wait_recv()
        add_to(parts, first, 2, up1[q])
        ups2.append(net.send(blocks(parts, first, B), up2.at[q], y=1))
        first = product(3, FWD_ORDER[q])
        downs1[q].wait_recv()
        add_to(parts, first + 2, 2, down1[q])
        downs2.append(net.send(blocks(parts, first, B), down2.at[q], y=3))

    def third(q):
        first = product(0, FWD_ORDER[q])
        ups2[q].wait_recv()
        downs2[q].wait_recv()
        here = parts[pl.ds(first, B)].astype(F32) + up2[q].astype(F32) + down2[q].astype(F32)
        if q < 3:
            zsend[q] = here.astype(BF)
            zs.append(net.send(zsend.at[q], zrecv.at[q], z=FWD_ORDER[q]))
        else:
            total[...] = here

    second(0)
    second(1)
    second(2)
    third(0)
    second(3)
    third(1)
    third(2)
    third(3)
    for copy in zs:
        copy.wait_recv()

    got_rowdeg.wait()
    got_weight.wait()
    got_cot.wait()
    row_scale = lax.rsqrt(rowdeg_ref[...].astype(F32))
    weight = weight_ref[...]
    lean = math.sqrt(2.0 / math.pi)
    for t in range(B):
        rows = pl.ds(t * T, T)
        aggregate = total[t]
        for q in range(3):
            aggregate = aggregate + zrecv[q, t].astype(F32)
        smoothed = (aggregate * down_rows(row_scale, t)).astype(BF)
        pre = jnp.dot(smoothed, weight, preferred_element_type=F32)
        square = pre * pre
        slope = jnp.tanh(lean * pre * (1.0 + 0.044715 * square))
        gate = 0.5 * (1.0 + slope)
        hidden_ref[rows, :] = (pre * gate).astype(BF)
        steep = gate + 0.5 * pre * (1.0 - slope * slope) * (lean * (1.0 + 3.0 * 0.044715 * square))
        grad_pre = (cot_ref[rows, :].astype(F32) * steep).astype(BF)
        spread = lax.dot_general(weight, grad_pre, (((1,), (1,)), ((), ())), preferred_element_type=F32)
        gpanel[col * B + t] = (spread * row_scale[t : t + 1, :]).astype(BF)
        outer = lax.dot_general(smoothed, grad_pre, (((0,), (0,)), ((), ())), preferred_element_type=F32)
        if t == 0:
            wlocal[...] = outer
        else:
            wlocal[...] += outer

    put_hidden = move(hidden_ref, hidden_hbm)

    def grads_at(y, z, first=0, count=B):
        place = mod4(my + y) * 4 + masked(ml, z)
        return blocks(gpanel, place * B + first, count)

    def hand_on(dy, dz, first, count, **shift):
        ref = grads_at(dy, dz, first, count)
        return net.send(ref, ref, **shift)

    def back(y, z):
        first = (mod4(my + y) * 4 + masked(ml, z)) * B

        def tile(r):
            grads = gpanel[r]
            for k in range(0, K, 2):
                slot = r * K + k
                rhs = jnp.concatenate([entries[r, k], entries[r, k + 1]], axis=1)
                both = jnp.dot(grads, rhs, preferred_element_type=F32)
                one = chain[places[k, r]] + both[:, :T]
                two = chain[places[k + 1, r]] + both[:, T:]
                chain[slot] = one
                chain[slot + 1] = two

        for t in range(B):
            tile(first + t)

    gups, gdowns, fups, fdowns = [], [], [], []

    def along(mask):
        gups.append(hand_on(0, mask, 0, B, y=1))
        gdowns.append(hand_on(0, mask, 0, B, y=3))

    def forward(mask):
        gups[mask].wait_recv()
        fups.append(hand_on(-1, mask, 0, 2, y=1))
        gdowns[mask].wait_recv()
        fdowns.append(hand_on(1, mask, 2, 2, y=3))

    along(0)
    gz = [None] + [hand_on(0, 0, 0, B, z=mask) for mask in (1, 2, 3)]
    wys = [
        net.send(wlocal.at[pl.ds(mod4(my + d) * 32, 32)], wy.at[d - 1], y=d) for d in (1, 2, 3)
    ]
    back(0, 0)
    gz[1].wait_recv()
    along(1)
    back(0, 1)
    forward(0)
    back(3, 0)
    back(1, 0)
    gz[2].wait_recv()
    along(2)
    back(0, 2)
    gz[3].wait_recv()
    along(3)
    back(0, 3)
    forward(1)
    for copy in wys:
        copy.wait_recv()
    wz[3] = wlocal[pl.ds(my * 32, 32), :] + wy[0] + wy[1] + wy[2]
    wzs = [
        net.send(wz.at[3, pl.ds(masked(ml, m) * 8, 8)], wz.at[m - 1, pl.ds(0, 8)], z=m) for m in (1, 2, 3)
    ]
    back(3, 1)
    back(1, 1)
    forward(2)
    back(3, 2)
    back(1, 2)
    forward(3)
    back(3, 3)
    back(1, 3)
    for copy in wzs:
        copy.wait_recv()
    wx[mx] = wz[3, pl.ds(ml * 8, 8), :] + wz[0, :8, :] + wz[1, :8, :] + wz[2, :8, :]
    wxs = [net.send(wx.at[mx], wx.at[mx], x=d) for d in (1, 2, 3)]
    for mask in range(4):
        fups[mask].wait_recv()
        fdowns[mask].wait_recv()
        back(2, mask)
    for copy in wxs:
        copy.wait_recv()
    wc[0] = wx[0] + wx[1] + wx[2] + wx[3]
    wcs = net.send(wc.at[0], wc.at[1], core=1)

    def column(half, x, core):
        return (lax.rem(mz + half, 2) * 8 + mod4(mx + x) * 2 + lax.rem(mc + core, 2)) * B

    order = [(half, x) for half in (1, 0) for x in (2, 1, 3, 0)]
    cores = []
    for n, (half, x) in enumerate(order):
        first = column(half, x, 1)
        for t in range(B):
            csend[n, t] = chain[places[LAST, first + t]].astype(BF)
        cores.append(net.send(csend.at[n], crecv.at[n], core=1))
    near, far = {}, {}

    def chip_sum(n):
        half, x = order[n]
        first = column(half, x, 0)
        cores[n].wait_recv()
        for t in range(B):
            xsum[n, t] = (chain[places[LAST, first + t]] + crecv[n, t].astype(F32)).astype(BF)

    def opposite(h, t):
        near[h, t] = (
            net.send(blocks(xsum.at[4 * h], t, 1), blocks(xup1.at[h], t // 2, 1), x=1),
            net.send(blocks(xsum.at[4 * h], t + 1, 1), blocks(xdown1.at[h], t // 2, 1), x=3),
        )

    def beside(h, t):
        up, down = near[h, t]
        up.wait_recv()
        right, left = xsum.at[4 * h + 1], xsum.at[4 * h + 2]
        right[t] = (right[t].astype(F32) + xup1[h, t // 2].astype(F32)).astype(BF)
        up = net.send(blocks(right, t, 2), blocks(xup2.at[h], t, 2), x=1)
        down.wait_recv()
        left[t + 1] = (left[t + 1].astype(F32) + xdown1[h, t // 2].astype(F32)).astype(BF)
        far[h, t] = (up, net.send(blocks(left, t, 2), blocks(xdown2.at[h], t, 2), x=3))

    def gathered(h, t):
        for copy in far[h, t]:
            copy.wait_recv()
        two = pl.ds(t, 2)
        return xsum[4 * h + 3, two].astype(F32) + xup2[h, two].astype(F32) + xdown2[h, two].astype(F32)

    across = []

    def cross(t):
        hsend[pl.ds(t, 2)] = gathered(0, t).astype(BF)
        across.append(net.send(blocks(hsend, t, 2), blocks(hrecv, t, 2), half=1))

    chip_sum(0)
    opposite(0, 0)
    opposite(0, 2)
    chip_sum(1)
    chip_sum(2)
    beside(0, 0)
    beside(0, 2)
    chip_sum(4)
    opposite(1, 0)
    opposite(1, 2)
    wcs.wait_recv()
    wh[0] = wc[0] + wc[1]
    whs = net.send(wh.at[0], wh.at[1], half=1)
    chip_sum(3)
    cross(0)
    chip_sum(5)
    chip_sum(6)
    beside(1, 0)
    cross(2)
    beside(1, 2)
    chip_sum(7)

    whs.wait_recv()
    wrows = my * 32 + ml * 8
    wfull[pl.ds(wrows, 8), :] = (wh[0] + wh[1]) * grad_scale
    wzs2 = [
        net.send(wfull.at[pl.ds(wrows, 8)], wfull.at[pl.ds(wrows, 8)], z=d) for d in (1, 2, 3)
    ]

    for copy in wzs2:
        copy.wait_recv()
    wband = wfull.at[pl.ds(my * 32, 32)]
    wys2 = [net.send(wband, wband, y=d) for d in (1, 2, 3)]
    for t, copy in zip(halves, across):
        here = gathered(1, t)
        copy.wait_recv()
        for u in range(2):
            tile = here[u] + hrecv[t + u].astype(F32)
            fgrad_ref[pl.ds((t + u) * T, T), :] = (tile * col_scale[t + u : t + u + 1, :]).T.astype(BF)
    put_fgrad = move(fgrad_ref, fgrad_hbm)
    for copy in wys2:
        copy.wait_recv()
    put_wgrad = move(wfull, wgrad_hbm)
    for copy in net.made:
        copy.wait_send()
    for put in (put_hidden, put_fgrad, put_wgrad):
        put.wait()


def find_places(cols_ref, mask_ref, found, my, ml):
    square = (TILES, TILES)

    def turn_of(r):
        dy = mod4(r // 16 - my)
        z = lax.rem(r // 4, 4)
        turn = jnp.zeros_like(r)
        for n, (y, mask) in enumerate(TURNS):
            turn = jnp.where((dy == y) & (z == masked(ml, mask)), n, turn)
        return turn * B + lax.rem(r, B)

    over = lax.broadcasted_iota(jnp.int32, square, 1)
    down = lax.broadcasted_iota(jnp.int32, square, 0)
    turn_over = turn_of(over[:1])
    turn_down = turn_of(down)
    index = [jnp.where(mask_ref[k] > 0, cols_ref[k], ZERO) for k in range(K)]
    index_down = [jnp.broadcast_to(index[k], square).T for k in range(K)]
    key_down = [turn_down * 512 + down * K + k for k in range(K)]

    def slot_of(key, live):
        return jnp.where(live & (key >= 0), lax.rem(key, 512), EMPTY)

    ahead = turn_down < turn_over
    for k in range(K):
        best = jnp.full(square, -1, jnp.int32)
        for j in range(K):
            best = jnp.maximum(best, jnp.where(index_down[j] == index[k], key_down[j], -1))
        key = jnp.max(jnp.where(ahead, best, -1), axis=0, keepdims=True)
        found[k : k + 1, :TILES] = slot_of(key, index[k] < ZERO)
        found[INDEX + k : INDEX + k + 1, :TILES] = index[k]
    best = jnp.full(square, -1, jnp.int32)
    for j in range(K):
        best = jnp.maximum(best, jnp.where(index_down[j] == over, key_down[j], -1))
    key = jnp.max(best, axis=0, keepdims=True)
    found[LAST : LAST + 1, :TILES] = slot_of(key, key >= 0)


def finish(*refs):
    n = len(refs) // 2
    for source, target in zip(refs[:n], refs[n:]):
        target[...] = source[...]


def body(features, weight, row_degree, col_degree, tile_cols, slot_mask, tile_entries, cotangent):
    anywhere = pl.BlockSpec(memory_space=pl.ANY)
    vmem = pl.BlockSpec(memory_space=pltpu.VMEM)
    nodes, hidden_width = cotangent.shape
    count = nodes * lax.axis_size("row") * lax.axis_size("col")
    grad_scale = 1.0 / (32.0 * math.sqrt(count))

    def tiles(*lead, dtype=BF):
        return pltpu.VMEM((*lead, T, T), dtype)

    def wide(*shape):
        return pltpu.VMEM((*shape, hidden_width), F32)

    shapes = (
        jax.ShapeDtypeStruct((nodes, hidden_width), BF),
        jax.ShapeDtypeStruct((T, hidden_width), F32),
        jax.ShapeDtypeStruct((nodes, T), BF),
    )
    results = pl.pallas_call(
        functools.partial(kernel, grad_scale),
        out_shape=shapes,
        in_specs=[anywhere] * 8,
        out_specs=(anywhere,) * 3,
        scratch_shapes=[
            pltpu.VMEM((K, 1, TILES), jnp.int32), pltpu.VMEM((K, 1, TILES), jnp.int32),
            pltpu.VMEM((nodes, T), BF), pltpu.VMEM((T, hidden_width), BF),
            pltpu.VMEM((B, T), jnp.int32), pltpu.VMEM((B, T), jnp.int32),
            pltpu.VMEM((nodes, hidden_width), BF), pltpu.VMEM((nodes, hidden_width), BF), pltpu.VMEM((nodes, T), BF),
            pltpu.VMEM((16, 128), jnp.int32), pltpu.SMEM((16, 128), jnp.int32),
            tiles(TILES, K), tiles(TILES + 1), tiles(TILES),
            tiles(4, 2), tiles(4, 2), tiles(4, B), tiles(4, B), tiles(3, B), tiles(3, B), tiles(B, dtype=F32),
            tiles(TILES), tiles(SLOTS + 1, dtype=F32),
            wide(T), wide(3, 32), wide(4, 32), wide(4, 8), wide(2, 8), wide(2, 8), wide(T),
            tiles(8, B), tiles(8, B), tiles(8, B),
            tiles(2, 2), tiles(2, 2), tiles(2, B), tiles(2, B), tiles(B), tiles(B),
            pltpu.SemaphoreType.DMA((N_LOADS,)),
            pltpu.SemaphoreType.DMA((16,)),
            pltpu.SemaphoreType.DMA((N_COPIES,)),
            pltpu.SemaphoreType.DMA((N_COPIES,)),
        ],
        compiler_params=pltpu.CompilerParams(
            collective_id=0, has_side_effects=True, vmem_limit_bytes=60 * 1024 * 1024
        ),
        name="graph_layer",
    )(
        tile_cols.transpose(2, 1, 0), slot_mask.transpose(2, 1, 0), tile_entries.reshape(TILES, K, T, T),
        features, weight, row_degree.reshape(B, T), col_degree.reshape(B, T), cotangent,
    )
    return pl.pallas_call(
        finish,
        out_shape=shapes,
        in_specs=[vmem] * 3,
        out_specs=(vmem,) * 3,
        name="results",
    )(*results)


def solution(mesh):
    return jax.shard_map(
        body,
        mesh=mesh,
        in_specs=(
            P(("col", "row"), None),
            P(),
            P(("row", "col")),
            P(("col", "row")),
            P("row", "col", None),
            P("row", "col", None),
            P("row", "col", None, None, None),
            P(("row", "col"), None),
        ),
        out_specs=(P(("row", "col"), None), P(), P(("col", "row"), None)),
        check_vma=False,
    )
```

```python
import functools
import math

import jax
import jax.numpy as jnp
from jax import lax
from jax.experimental import pallas as pl
from jax.experimental.pallas import tpu as pltpu
from jax.sharding import PartitionSpec as P

MESH = pl.DeviceIdType.MESH
BF = jnp.bfloat16
F32 = jnp.float32

T = 128
B = 4
K = 6
TILES = 64
SLOTS = TILES * K
EMPTY = SLOTS
ZERO = TILES
FWD_ORDER = (3, 2, 1, 0)
TURNS = ((0, 0, 0), (0, 0, 1), (1, 0, 0), (0, 3, 0), (0, 1, 0), (0, 0, 2), (0, 0, 3), (1, 0, 1))
TURNS += ((0, 3, 1), (0, 1, 1), (1, 3, 0), (1, 1, 0), (1, 0, 2), (1, 0, 3))
TURNS += ((0, 3, 2), (0, 1, 2), (0, 3, 3), (0, 1, 3), (1, 3, 1), (1, 1, 1))
TURNS += ((1, 3, 2), (1, 1, 2), (1, 3, 3), (1, 1, 3))
TURNS += tuple((half, 2, mask) for half in (0, 1) for mask in range(4))
N_COPIES = 224
N_LOADS = 8
LAST = 6
INDEX = 8


def coords():
    row, col = lax.axis_index("row"), lax.axis_index("col")
    return row // 8, lax.rem(row // 2, 4), lax.rem(row, 2), col // 4, lax.rem(col, 4)


def mod4(value):
    return lax.rem(value + 8, 4)


def masked(z, mask):
    return (z, z + 1 - 2 * lax.rem(z, 2), mod4(z + 2), 3 - z)[mask]


class Copies:
    def __init__(self, send_sems, recv_sems):
        self.sems = (send_sems, recv_sems)
        self.made = []
        self.place = coords()

    def device(self, x=0, y=0, z=0, core=0, half=0):
        mz, mx, mc, my, ml = self.place
        row = lax.rem(mz + half, 2) * 8 + mod4(mx + x) * 2 + lax.rem(mc + core, 2)
        return (row, mod4(my + y) * 4 + masked(ml, z))

    def send(self, src, dst, **shift):
        n = len(self.made)
        copy = pltpu.make_async_remote_copy(
            src_ref=src,
            dst_ref=dst,
            send_sem=self.sems[0].at[n],
            recv_sem=self.sems[1].at[n],
            device_id=self.device(**shift),
            device_id_type=MESH,
        )
        copy.start()
        self.made.append(copy)
        return copy


PEERS = (
    [dict(x=1), dict(x=3), dict(x=2)]
    + [dict(y=1), dict(y=3), dict(y=2)]
    + [dict(z=1), dict(z=3), dict(z=2)]
    + [dict(core=1), dict(half=1)]
)


def blocks(ref, first, count):
    return ref.at[pl.ds(first, count)]


def kernel(
    grad_scale,
    cols_hbm, mask_hbm, entries_hbm, feat_hbm, weight_hbm, rowdeg_hbm, coldeg_hbm, cot_hbm,
    hidden_hbm, wgrad_hbm, fgrad_hbm,
    cols_ref, mask_ref, feat_ref, weight_ref, rowdeg_ref, coldeg_ref, cot_ref, hidden_ref, fgrad_ref, found, places,
    entries, panel, parts, up1, down1, up2, down2, zsend, zrecv, total,
    gpanel, chain, wlocal, wy, wz, wx, wc, wh, wfull,
    csend, crecv, xsum, xup1, xdown1, xup2, xdown2, hsend, hrecv,
    load_sems, io_sems, send_sems, recv_sems,
):
    net = Copies(send_sems, recv_sems)
    mz, mx, mc, my, ml = net.place
    row, col = lax.axis_index("row"), lax.axis_index("col")

    barrier = pltpu.get_barrier_semaphore()
    for shift in PEERS:
        pl.semaphore_signal(barrier, inc=1, device_id=net.device(**shift), device_id_type=MESH)

    moves = []

    def move(src, dst):
        copy = pltpu.make_async_copy(src, dst, io_sems.at[len(moves)])
        copy.start()
        moves.append(copy)
        return copy

    got_coldeg = move(coldeg_hbm, coldeg_ref)
    got_feat = move(feat_hbm, feat_ref)
    got_cols = move(cols_hbm, cols_ref)
    got_mask = move(mask_hbm, mask_ref)
    got_rowdeg = move(rowdeg_hbm, rowdeg_ref)
    got_weight = move(weight_hbm, weight_ref)
    got_cot = move(cot_hbm, cot_ref)
    share = TILES // N_LOADS
    loads = []
    for n in range(N_LOADS):
        load = pltpu.make_async_copy(
            entries_hbm.at[pl.ds(n * share, share)], entries.at[pl.ds(n * share, share)], load_sems.at[n]
        )
        load.start()
        loads.append(load)

    got_coldeg.wait()
    got_feat.wait()
    col_scale = lax.rsqrt(coldeg_ref[...].astype(F32))

    def down_rows(scale, t):
        return jnp.broadcast_to(scale[t : t + 1, :], (T, T)).T

    mine = row * B
    for t in range(B):
        panel[mine + t] = (feat_ref[pl.ds(t * T, T), :].astype(F32) * down_rows(col_scale, t)).astype(BF)
    panel[ZERO] = jnp.zeros((T, T), BF)
    chain[EMPTY] = jnp.zeros((T, T), F32)
    pl.semaphore_wait(barrier, len(PEERS))

    def panel_at(half, x, first=0, count=B):
        place = lax.rem(mz + half, 2) * 8 + mod4(mx + x) * 2 + mc
        return blocks(panel, place * B + first, count)

    def pass_on(part, dx, first, count, **shift):
        ref = panel_at(part, dx, first, count)
        return net.send(ref, ref, **shift)

    from_core = []

    def share_core(half, x, first=0, count=B):
        from_core.append(pass_on(half, x, first, count, core=1))

    halves = (0, 2)
    over = [pass_on(0, 0, t, 2, half=1) for t in halves]
    right = pass_on(0, 0, 0, B, x=1)
    left = pass_on(0, 0, 0, B, x=3)
    share_core(0, 0)

    got_cols.wait()
    got_mask.wait()
    find_places(cols_ref, mask_ref, found, my, ml)
    got_places = move(found, places)

    right.wait_recv()
    fright = pass_on(0, -1, 0, 2, x=1)
    left.wait_recv()
    fleft = pass_on(0, 1, 2, 2, x=3)
    share_core(0, -1)
    share_core(0, 1)
    others = []
    for t, copy in zip(halves, over):
        copy.wait_recv()
        others.append([pass_on(1, 0, t, 2, x=d) for d in (1, 3, 2)])
        share_core(1, 0, t, 2)
    fright.wait_recv()
    fleft.wait_recv()
    share_core(0, 2)
    for t, copies in zip(halves, others):
        for copy, d in zip(copies, (-1, 1, 2)):
            copy.wait_recv()
            share_core(1, d, t, 2)
    for load in loads:
        load.wait()
    for copy in from_core:
        copy.wait_recv()
    got_places.wait()

    def product(half, y, z):
        first = (mod4(my + y) * 4 + masked(ml, z)) * B + 2 * half

        def tile(r):
            acc = jnp.zeros((T, T), F32)
            for k in range(0, K, 2):
                lhs = jnp.concatenate([entries[r, k], entries[r, k + 1]], axis=1)
                rhs = jnp.concatenate(
                    [panel[places[INDEX + k, r]], panel[places[INDEX + k + 1, r]]], axis=0
                )
                acc = acc + jnp.dot(lhs, rhs, preferred_element_type=F32)
            parts[r] = acc.astype(BF)

        for t in range(2):
            tile(first + t)
        return first

    def add_to(ref, first, count, other):
        where = pl.ds(first, count)
        ref[where] = (ref[where].astype(F32) + other.astype(F32)).astype(BF)

    ups1, downs1, ups2, downs2, zs = {}, {}, {}, {}, {}

    def first(h, pair):
        for q, place in [(q, product(h, 2, FWD_ORDER[q])) for q in pair]:
            ups1[h, q] = net.send(blocks(parts, place, 1), blocks(up1.at[q], h, 1), y=1)
            downs1[h, q] = net.send(blocks(parts, place + 1, 1), blocks(down1.at[q], h, 1), y=3)

    def second(h, q):
        two = pl.ds(2 * h, 2)
        right, left = product(h, 1, FWD_ORDER[q]), product(h, 3, FWD_ORDER[q])
        ups1[h, q].wait_recv()
        add_to(parts, right, 1, up1[q, pl.ds(h, 1)])
        ups2[h, q] = net.send(blocks(parts, right, 2), up2.at[q, two], y=1)
        downs1[h, q].wait_recv()
        add_to(parts, left + 1, 1, down1[q, pl.ds(h, 1)])
        downs2[h, q] = net.send(blocks(parts, left, 2), down2.at[q, two], y=3)

    def own(h):
        for q in range(4):
            product(h, 0, FWD_ORDER[q])

    def third(h, q):
        two = pl.ds(2 * h, 2)
        place = (my * 4 + masked(ml, FWD_ORDER[q])) * B + 2 * h
        ups2[h, q].wait_recv()
        downs2[h, q].wait_recv()
        here = parts[pl.ds(place, 2)].astype(F32) + up2[q, two].astype(F32) + down2[q, two].astype(F32)
        if q < 3:
            zsend[q, two] = here.astype(BF)
            zs[h, q] = net.send(zsend.at[q, two], zrecv.at[q, two], z=FWD_ORDER[q])
        else:
            total[two] = here

    got_rowdeg.wait()
    got_weight.wait()
    got_cot.wait()
    row_scale = lax.rsqrt(rowdeg_ref[...].astype(F32))
    weight = weight_ref[...]
    lean = math.sqrt(2.0 / math.pi)
    def dense(h):
        for q in range(3):
            zs[h, q].wait_recv()
        for t in (2 * h, 2 * h + 1):
            rows = pl.ds(t * T, T)
            aggregate = total[t]
            for q in range(3):
                aggregate = aggregate + zrecv[q, t].astype(F32)
            smoothed = (aggregate * down_rows(row_scale, t)).astype(BF)
            pre = jnp.dot(smoothed, weight, preferred_element_type=F32)
            square = pre * pre
            slope = jnp.tanh(lean * pre * (1.0 + 0.044715 * square))
            gate = 0.5 * (1.0 + slope)
            hidden_ref[rows, :] = (pre * gate).astype(BF)
            steep = gate + 0.5 * pre * (1.0 - slope * slope) * (lean * (1.0 + 3.0 * 0.044715 * square))
            grad_pre = (cot_ref[rows, :].astype(F32) * steep).astype(BF)
            spread = lax.dot_general(weight, grad_pre, (((1,), (1,)), ((), ())), preferred_element_type=F32)
            gpanel[col * B + t] = (spread * row_scale[t : t + 1, :]).astype(BF)
            outer = lax.dot_general(smoothed, grad_pre, (((0,), (0,)), ((), ())), preferred_element_type=F32)
            if t == 0:
                wlocal[...] = outer
            else:
                wlocal[...] += outer

    def grads_at(y, z, first=0, count=B):
        place = mod4(my + y) * 4 + masked(ml, z)
        return blocks(gpanel, place * B + first, count)

    def hand_on(dy, dz, first, count, **shift):
        ref = grads_at(dy, dz, first, count)
        return net.send(ref, ref, **shift)

    def back(half, y, z):
        first = (mod4(my + y) * 4 + masked(ml, z)) * B + 2 * half

        def tile(r):
            grads = gpanel[r]
            for k in range(0, K, 2):
                slot = r * K + k
                rhs = jnp.concatenate([entries[r, k], entries[r, k + 1]], axis=1)
                both = jnp.dot(grads, rhs, preferred_element_type=F32)
                one = chain[places[k, r]] + both[:, :T]
                two = chain[places[k + 1, r]] + both[:, T:]
                chain[slot] = one
                chain[slot + 1] = two

        for t in range(2):
            tile(first + t)

    gups, gdowns, fups, fdowns, gz = {}, {}, {}, {}, {}

    def along(h, mask):
        if mask > 0:
            gz[h, mask].wait_recv()
        gups[h, mask] = hand_on(0, mask, 2 * h, 2, y=1)
        gdowns[h, mask] = hand_on(0, mask, 2 * h, 2, y=3)

    def forward(h, mask):
        gups[h, mask].wait_recv()
        fups[h, mask] = hand_on(-1, mask, 2 * h, 1, y=1)
        gdowns[h, mask].wait_recv()
        fdowns[h, mask] = hand_on(1, mask, 2 * h + 1, 1, y=3)

    def over_z(h):
        for mask in (1, 2, 3):
            gz[h, mask] = hand_on(0, 0, 2 * h, 2, z=mask)

    def beside_back(h, mask):
        back(h, 3, mask)
        back(h, 1, mask)

    first(0, (0, 1))
    first(0, (2, 3))
    second(0, 0)
    second(0, 1)
    first(1, (0, 1))
    first(1, (2, 3))
    second(0, 2)
    second(0, 3)
    own(0)
    third(0, 0)
    second(1, 0)
    third(0, 1)
    second(1, 1)
    third(0, 2)
    second(1, 2)
    third(0, 3)
    second(1, 3)
    own(1)
    third(1, 0)
    dense(0)
    along(0, 0)
    third(1, 1)
    third(1, 2)
    over_z(0)
    third(1, 3)
    back(0, 0, 0)
    along(0, 1)
    dense(1)
    along(1, 0)
    over_z(1)
    put_hidden = move(hidden_ref, hidden_hbm)
    wys = [
        net.send(wlocal.at[pl.ds(mod4(my + d) * 32, 32)], wy.at[d - 1], y=d) for d in (1, 2, 3)
    ]
    forward(0, 0)
    back(0, 0, 1)
    back(1, 0, 0)
    along(0, 2)
    along(0, 3)
    beside_back(0, 0)
    back(0, 0, 2)
    back(0, 0, 3)
    along(1, 1)
    forward(0, 1)
    forward(1, 0)
    back(1, 0, 1)
    beside_back(0, 1)
    beside_back(1, 0)
    along(1, 2)
    along(1, 3)
    for copy in wys:
        copy.wait_recv()
    wz[3] = wlocal[pl.ds(my * 32, 32), :] + wy[0] + wy[1] + wy[2]
    wzs = [
        net.send(wz.at[3, pl.ds(masked(ml, m) * 8, 8)], wz.at[m - 1, pl.ds(0, 8)], z=m) for m in (1, 2, 3)
    ]
    back(1, 0, 2)
    back(1, 0, 3)
    forward(0, 2)
    forward(0, 3)
    beside_back(0, 2)
    beside_back(0, 3)
    forward(1, 1)
    forward(1, 2)
    beside_back(1, 1)
    beside_back(1, 2)
    for copy in wzs:
        copy.wait_recv()
    wx[mx] = wz[3, pl.ds(ml * 8, 8), :] + wz[0, :8, :] + wz[1, :8, :] + wz[2, :8, :]
    wxs = [net.send(wx.at[mx], wx.at[mx], x=d) for d in (1, 2, 3)]
    forward(1, 3)
    beside_back(1, 3)
    for mask in range(4):
        fups[0, mask].wait_recv()
        fdowns[0, mask].wait_recv()
    for mask in range(4):
        back(0, 2, mask)
    for copy in wxs:
        copy.wait_recv()
    wc[0] = wx[0] + wx[1] + wx[2] + wx[3]
    wcs = net.send(wc.at[0], wc.at[1], core=1)
    for pair in ((0, 1), (2, 3)):
        for mask in pair:
            fups[1, mask].wait_recv()
            fdowns[1, mask].wait_recv()
        for mask in pair:
            back(1, 2, mask)
    wcs.wait_recv()
    wh[0] = wc[0] + wc[1]
    whs = net.send(wh.at[0], wh.at[1], half=1)

    def column(half, x, core):
        return (lax.rem(mz + half, 2) * 8 + mod4(mx + x) * 2 + lax.rem(mc + core, 2)) * B

    order = [(half, x) for half in (1, 0) for x in (2, 1, 3, 0)]
    cores = []
    for n, (half, x) in enumerate(order):
        first = column(half, x, 1)
        for t in range(B):
            csend[n, t] = chain[places[LAST, first + t]].astype(BF)
        cores.append(net.send(csend.at[n], crecv.at[n], core=1))
    near, far = {}, {}

    def chip_sum(n):
        half, x = order[n]
        first = column(half, x, 0)
        cores[n].wait_recv()
        for t in range(B):
            xsum[n, t] = (chain[places[LAST, first + t]] + crecv[n, t].astype(F32)).astype(BF)

    def opposite(h, t):
        near[h, t] = (
            net.send(blocks(xsum.at[4 * h], t, 1), blocks(xup1.at[h], t // 2, 1), x=1),
            net.send(blocks(xsum.at[4 * h], t + 1, 1), blocks(xdown1.at[h], t // 2, 1), x=3),
        )

    def beside(h, t):
        up, down = near[h, t]
        up.wait_recv()
        right, left = xsum.at[4 * h + 1], xsum.at[4 * h + 2]
        right[t] = (right[t].astype(F32) + xup1[h, t // 2].astype(F32)).astype(BF)
        up = net.send(blocks(right, t, 2), blocks(xup2.at[h], t, 2), x=1)
        down.wait_recv()
        left[t + 1] = (left[t + 1].astype(F32) + xdown1[h, t // 2].astype(F32)).astype(BF)
        far[h, t] = (up, net.send(blocks(left, t, 2), blocks(xdown2.at[h], t, 2), x=3))

    def gathered(h, t):
        for copy in far[h, t]:
            copy.wait_recv()
        two = pl.ds(t, 2)
        return xsum[4 * h + 3, two].astype(F32) + xup2[h, two].astype(F32) + xdown2[h, two].astype(F32)

    across = []

    def cross(t):
        hsend[pl.ds(t, 2)] = gathered(0, t).astype(BF)
        across.append(net.send(blocks(hsend, t, 2), blocks(hrecv, t, 2), half=1))

    chip_sum(0)
    opposite(0, 0)
    opposite(0, 2)
    chip_sum(1)
    chip_sum(2)
    beside(0, 0)
    beside(0, 2)
    whs.wait_recv()
    wrows = my * 32 + ml * 8
    wfull[pl.ds(wrows, 8), :] = (wh[0] + wh[1]) * grad_scale
    wzs2 = [
        net.send(wfull.at[pl.ds(wrows, 8)], wfull.at[pl.ds(wrows, 8)], z=m) for m in (1, 2, 3)
    ]
    chip_sum(4)
    opposite(1, 0)
    opposite(1, 2)
    chip_sum(3)
    cross(0)
    cross(2)
    chip_sum(5)
    chip_sum(6)
    beside(1, 0)
    beside(1, 2)
    chip_sum(7)
    for copy in wzs2:
        copy.wait_recv()
    wband = wfull.at[pl.ds(my * 32, 32)]
    wys2 = [net.send(wband, wband, y=d) for d in (1, 2, 3)]
    for t, copy in zip(halves, across):
        here = gathered(1, t)
        copy.wait_recv()
        for u in range(2):
            tile = here[u] + hrecv[t + u].astype(F32)
            fgrad_ref[pl.ds((t + u) * T, T), :] = (tile * col_scale[t + u : t + u + 1, :]).T.astype(BF)
    put_fgrad = move(fgrad_ref, fgrad_hbm)
    for copy in wys2:
        copy.wait_recv()
    put_wgrad = move(wfull, wgrad_hbm)
    for copy in net.made:
        copy.wait_send()
    for put in (put_hidden, put_fgrad, put_wgrad):
        put.wait()


def find_places(cols_ref, mask_ref, found, my, ml):
    square = (TILES, TILES)

    def turn_of(r):
        dy = mod4(r // 16 - my)
        z = lax.rem(r // 4, 4)
        part = lax.rem(r // 2, 2)
        turn = jnp.zeros_like(r)
        for n, (half, y, mask) in enumerate(TURNS):
            turn = jnp.where((part == half) & (dy == y) & (z == masked(ml, mask)), n, turn)
        return turn * 2 + lax.rem(r, 2)

    over = lax.broadcasted_iota(jnp.int32, square, 1)
    down = lax.broadcasted_iota(jnp.int32, square, 0)
    turn_over = turn_of(over[:1])
    turn_down = turn_of(down)
    index = [jnp.where(mask_ref[k] > 0, cols_ref[k], ZERO) for k in range(K)]
    index_down = [jnp.broadcast_to(index[k], square).T for k in range(K)]
    key_down = [turn_down * 512 + down * K + k for k in range(K)]

    def slot_of(key, live):
        return jnp.where(live & (key >= 0), lax.rem(key, 512), EMPTY)

    ahead = turn_down < turn_over
    for k in range(K):
        best = jnp.full(square, -1, jnp.int32)
        for j in range(K):
            best = jnp.maximum(best, jnp.where(index_down[j] == index[k], key_down[j], -1))
        key = jnp.max(jnp.where(ahead, best, -1), axis=0, keepdims=True)
        found[k : k + 1, :TILES] = slot_of(key, index[k] < ZERO)
        found[INDEX + k : INDEX + k + 1, :TILES] = index[k]
    best = jnp.full(square, -1, jnp.int32)
    for j in range(K):
        best = jnp.maximum(best, jnp.where(index_down[j] == over, key_down[j], -1))
    key = jnp.max(best, axis=0, keepdims=True)
    found[LAST : LAST + 1, :TILES] = slot_of(key, key >= 0)


def finish(*refs):
    n = len(refs) // 2
    for source, target in zip(refs[:n], refs[n:]):
        target[...] = source[...]


def body(features, weight, row_degree, col_degree, tile_cols, slot_mask, tile_entries, cotangent):
    anywhere = pl.BlockSpec(memory_space=pl.ANY)
    vmem = pl.BlockSpec(memory_space=pltpu.VMEM)
    nodes, hidden_width = cotangent.shape
    count = nodes * lax.axis_size("row") * lax.axis_size("col")
    grad_scale = 1.0 / (32.0 * math.sqrt(count))

    def tiles(*lead, dtype=BF):
        return pltpu.VMEM((*lead, T, T), dtype)

    def wide(*shape):
        return pltpu.VMEM((*shape, hidden_width), F32)

    shapes = (
        jax.ShapeDtypeStruct((nodes, hidden_width), BF),
        jax.ShapeDtypeStruct((T, hidden_width), F32),
        jax.ShapeDtypeStruct((nodes, T), BF),
    )
    results = pl.pallas_call(
        functools.partial(kernel, grad_scale),
        out_shape=shapes,
        in_specs=[anywhere] * 8,
        out_specs=(anywhere,) * 3,
        scratch_shapes=[
            pltpu.VMEM((K, 1, TILES), jnp.int32), pltpu.VMEM((K, 1, TILES), jnp.int32),
            pltpu.VMEM((nodes, T), BF), pltpu.VMEM((T, hidden_width), BF),
            pltpu.VMEM((B, T), jnp.int32), pltpu.VMEM((B, T), jnp.int32),
            pltpu.VMEM((nodes, hidden_width), BF), pltpu.VMEM((nodes, hidden_width), BF), pltpu.VMEM((nodes, T), BF),
            pltpu.VMEM((16, 128), jnp.int32), pltpu.SMEM((16, 128), jnp.int32),
            tiles(TILES, K), tiles(TILES + 1), tiles(TILES),
            tiles(4, 2), tiles(4, 2), tiles(4, B), tiles(4, B), tiles(3, B), tiles(3, B), tiles(B, dtype=F32),
            tiles(TILES), tiles(SLOTS + 1, dtype=F32),
            wide(T), wide(3, 32), wide(4, 32), wide(4, 8), wide(2, 8), wide(2, 8), wide(T),
            tiles(8, B), tiles(8, B), tiles(8, B),
            tiles(2, 2), tiles(2, 2), tiles(2, B), tiles(2, B), tiles(B), tiles(B),
            pltpu.SemaphoreType.DMA((N_LOADS,)),
            pltpu.SemaphoreType.DMA((16,)),
            pltpu.SemaphoreType.DMA((N_COPIES,)),
            pltpu.SemaphoreType.DMA((N_COPIES,)),
        ],
        compiler_params=pltpu.CompilerParams(
            collective_id=0, has_side_effects=True, vmem_limit_bytes=60 * 1024 * 1024
        ),
        name="graph_layer",
    )(
        tile_cols.transpose(2, 1, 0), slot_mask.transpose(2, 1, 0), tile_entries.reshape(TILES, K, T, T),
        features, weight, row_degree.reshape(B, T), col_degree.reshape(B, T), cotangent,
    )
    return pl.pallas_call(
        finish,
        out_shape=shapes,
        in_specs=[vmem] * 3,
        out_specs=(vmem,) * 3,
        name="results",
    )(*results)


def solution(mesh):
    return jax.shard_map(
        body,
        mesh=mesh,
        in_specs=(
            P(("col", "row"), None),
            P(),
            P(("row", "col")),
            P(("col", "row")),
            P("row", "col", None),
            P("row", "col", None),
            P("row", "col", None, None, None),
            P(("row", "col"), None),
        ),
        out_specs=(P(("row", "col"), None), P(), P(("col", "row"), None)),
        check_vma=False,
    )
```

```python
import functools
import math

import jax
import jax.numpy as jnp
from jax import lax
from jax.experimental import pallas as pl
from jax.experimental.pallas import tpu as pltpu
from jax.sharding import PartitionSpec as P

MESH = pl.DeviceIdType.MESH
BF = jnp.bfloat16
F32 = jnp.float32

T = 128
B = 4
K = 6
TILES = 64
SLOTS = TILES * K
EMPTY = SLOTS
ZERO = TILES
FWD_ORDER = (3, 2, 1, 0)
TURNS = ((0, 0, 0), (0, 0, 1), (1, 0, 0), (0, 3, 0), (0, 1, 0), (0, 0, 2), (0, 0, 3), (1, 0, 1))
TURNS += ((0, 3, 1), (0, 1, 1), (1, 3, 0), (1, 1, 0), (1, 0, 2), (1, 0, 3))
TURNS += ((0, 3, 2), (0, 1, 2), (0, 3, 3), (0, 1, 3), (1, 3, 1), (1, 1, 1))
TURNS += ((1, 3, 2), (1, 1, 2), (1, 3, 3), (1, 1, 3))
TURNS += tuple((half, 2, mask) for half in (0, 1) for mask in range(4))
N_COPIES = 224
N_LOADS = 8
LAST = 6
INDEX = 8


def coords():
    row, col = lax.axis_index("row"), lax.axis_index("col")
    return row // 8, lax.rem(row // 2, 4), lax.rem(row, 2), col // 4, lax.rem(col, 4)


def mod4(value):
    return lax.rem(value + 8, 4)


def masked(z, mask):
    return (z, z + 1 - 2 * lax.rem(z, 2), mod4(z + 2), 3 - z)[mask]


class Copies:
    def __init__(self, send_sems, recv_sems):
        self.sems = (send_sems, recv_sems)
        self.made = []
        self.seen = 0
        self.place = coords()
        self.devices = {}

    def device(self, **shift):
        key = tuple(sorted(shift.items()))
        if key not in self.devices:
            self.devices[key] = self.find(**shift)
        return self.devices[key]

    def find(self, x=0, y=0, z=0, core=0, half=0):
        mz, mx, mc, my, ml = self.place
        row = lax.rem(mz + half, 2) * 8 + mod4(mx + x) * 2 + lax.rem(mc + core, 2)
        return (row, mod4(my + y) * 4 + masked(ml, z))

    def send(self, src, dst, **shift):
        n = len(self.made)
        copy = pltpu.make_async_remote_copy(
            src_ref=src,
            dst_ref=dst,
            send_sem=self.sems[0].at[n],
            recv_sem=self.sems[1].at[n],
            device_id=self.device(**shift),
            device_id_type=MESH,
        )
        copy.start()
        self.made.append(copy)
        return copy

    def drain(self, count):
        for copy in self.made[self.seen : count]:
            copy.wait_send()
        self.seen = count


PEERS = (
    [dict(x=1), dict(x=3), dict(x=2)]
    + [dict(y=1), dict(y=3), dict(y=2)]
    + [dict(z=1), dict(z=3), dict(z=2)]
    + [dict(core=1), dict(half=1)]
)


def blocks(ref, first, count):
    return ref.at[pl.ds(first, count)]


def kernel(
    grad_scale,
    cols_hbm, mask_hbm, entries_hbm, feat_hbm, weight_hbm, rowdeg_hbm, coldeg_hbm, cot_hbm,
    hidden_hbm, wgrad_hbm, fgrad_hbm,
    cols_ref, mask_ref, feat_ref, weight_ref, rowdeg_ref, coldeg_ref, cot_ref, hidden_ref, fgrad_ref, found, places,
    entries, panel, parts, up1, down1, up2, down2, zsend, zrecv, total,
    gpanel, chain, wlocal, wy, wz, wx, wc, wh, wfull,
    csend, crecv, xsum, xup1, xdown1, xup2, xdown2, hsend, hrecv,
    load_sems, io_sems, send_sems, recv_sems,
):
    net = Copies(send_sems, recv_sems)
    mz, mx, mc, my, ml = net.place
    row, col = lax.axis_index("row"), lax.axis_index("col")

    barrier = pltpu.get_barrier_semaphore()
    for shift in PEERS:
        pl.semaphore_signal(barrier, inc=1, device_id=net.device(**shift), device_id_type=MESH)

    moves = []

    def move(src, dst):
        copy = pltpu.make_async_copy(src, dst, io_sems.at[len(moves)])
        copy.start()
        moves.append(copy)
        return copy

    got_coldeg = move(coldeg_hbm, coldeg_ref)
    got_feat = move(feat_hbm, feat_ref)
    got_cols = move(cols_hbm, cols_ref)
    got_mask = move(mask_hbm, mask_ref)
    got_rowdeg = move(rowdeg_hbm, rowdeg_ref)
    got_weight = move(weight_hbm, weight_ref)
    got_cot = move(cot_hbm, cot_ref)
    share = TILES // N_LOADS
    loads = []
    for n in range(N_LOADS):
        load = pltpu.make_async_copy(
            entries_hbm.at[pl.ds(n * share, share)], entries.at[pl.ds(n * share, share)], load_sems.at[n]
        )
        load.start()
        loads.append(load)

    got_coldeg.wait()
    got_feat.wait()
    col_scale = lax.rsqrt(coldeg_ref[...].astype(F32))

    def down_rows(scale, t):
        return jnp.broadcast_to(scale[t : t + 1, :], (T, T)).T

    mine = row * B
    for t in range(B):
        panel[mine + t] = (feat_ref[pl.ds(t * T, T), :].astype(F32) * down_rows(col_scale, t)).astype(BF)
    panel[ZERO] = jnp.zeros((T, T), BF)
    chain[EMPTY] = jnp.zeros((T, T), F32)
    pl.semaphore_wait(barrier, len(PEERS))

    def panel_at(half, x, first=0, count=B):
        place = lax.rem(mz + half, 2) * 8 + mod4(mx + x) * 2 + mc
        return blocks(panel, place * B + first, count)

    def pass_on(part, dx, first, count, **shift):
        ref = panel_at(part, dx, first, count)
        return net.send(ref, ref, **shift)

    from_core = []

    def share_core(half, x, first=0, count=B):
        from_core.append(pass_on(half, x, first, count, core=1))

    halves = (0, 2)
    over = [pass_on(0, 0, t, 2, half=1) for t in halves]
    right = pass_on(0, 0, 0, B, x=1)
    left = pass_on(0, 0, 0, B, x=3)
    share_core(0, 0)

    got_cols.wait()
    got_mask.wait()
    find_places(cols_ref, mask_ref, found, my, ml)
    got_places = move(found, places)

    right.wait_recv()
    fright = pass_on(0, -1, 0, 2, x=1)
    left.wait_recv()
    fleft = pass_on(0, 1, 2, 2, x=3)
    share_core(0, -1)
    share_core(0, 1)
    others = []
    for t, copy in zip(halves, over):
        copy.wait_recv()
        others.append([pass_on(1, 0, t, 2, x=d) for d in (1, 3, 2)])
        share_core(1, 0, t, 2)
    fright.wait_recv()
    fleft.wait_recv()
    share_core(0, 2)
    for t, copies in zip(halves, others):
        for copy, d in zip(copies, (-1, 1, 2)):
            copy.wait_recv()
            share_core(1, d, t, 2)
    for load in loads:
        load.wait()
    for copy in from_core:
        copy.wait_recv()
    got_places.wait()

    gathers = len(net.made)

    def product(half, y, z):
        first = (mod4(my + y) * 4 + masked(ml, z)) * B + 2 * half

        def tile(r):
            acc = jnp.zeros((T, T), F32)
            for k in range(0, K, 2):
                lhs = jnp.concatenate([entries[r, k], entries[r, k + 1]], axis=1)
                rhs = jnp.concatenate(
                    [panel[places[INDEX + k, r]], panel[places[INDEX + k + 1, r]]], axis=0
                )
                acc = acc + jnp.dot(lhs, rhs, preferred_element_type=F32)
            parts[r] = acc.astype(BF)

        for t in range(2):
            tile(first + t)
        return first

    def add_to(ref, first, count, other):
        where = pl.ds(first, count)
        ref[where] = (ref[where].astype(F32) + other.astype(F32)).astype(BF)

    ups1, downs1, ups2, downs2, zs = {}, {}, {}, {}, {}

    def first(h, pair):
        for q, place in [(q, product(h, 2, FWD_ORDER[q])) for q in pair]:
            ups1[h, q] = net.send(blocks(parts, place, 1), blocks(up1.at[q], h, 1), y=1)
            downs1[h, q] = net.send(blocks(parts, place + 1, 1), blocks(down1.at[q], h, 1), y=3)

    def second(h, q):
        two = pl.ds(2 * h, 2)
        right, left = product(h, 1, FWD_ORDER[q]), product(h, 3, FWD_ORDER[q])
        ups1[h, q].wait_recv()
        add_to(parts, right, 1, up1[q, pl.ds(h, 1)])
        ups2[h, q] = net.send(blocks(parts, right, 2), up2.at[q, two], y=1)
        downs1[h, q].wait_recv()
        add_to(parts, left + 1, 1, down1[q, pl.ds(h, 1)])
        downs2[h, q] = net.send(blocks(parts, left, 2), down2.at[q, two], y=3)

    def own(h):
        for q in range(4):
            product(h, 0, FWD_ORDER[q])

    def third(h, q):
        two = pl.ds(2 * h, 2)
        place = (my * 4 + masked(ml, FWD_ORDER[q])) * B + 2 * h
        ups2[h, q].wait_recv()
        downs2[h, q].wait_recv()
        here = parts[pl.ds(place, 2)].astype(F32) + up2[q, two].astype(F32) + down2[q, two].astype(F32)
        if q < 3:
            zsend[q, two] = here.astype(BF)
            zs[h, q] = net.send(zsend.at[q, two], zrecv.at[q, two], z=FWD_ORDER[q])
        else:
            total[two] = here

    got_rowdeg.wait()
    got_weight.wait()
    got_cot.wait()
    row_scale = lax.rsqrt(rowdeg_ref[...].astype(F32))
    weight = weight_ref[...]
    lean = math.sqrt(2.0 / math.pi)
    def dense(h):
        for q in range(3):
            zs[h, q].wait_recv()
        for t in (2 * h, 2 * h + 1):
            rows = pl.ds(t * T, T)
            aggregate = total[t]
            for q in range(3):
                aggregate = aggregate + zrecv[q, t].astype(F32)
            smoothed = (aggregate * down_rows(row_scale, t)).astype(BF)
            pre = jnp.dot(smoothed, weight, preferred_element_type=F32)
            square = pre * pre
            slope = jnp.tanh(lean * pre * (1.0 + 0.044715 * square))
            gate = 0.5 * (1.0 + slope)
            hidden_ref[rows, :] = (pre * gate).astype(BF)
            steep = gate + 0.5 * pre * (1.0 - slope * slope) * (lean * (1.0 + 3.0 * 0.044715 * square))
            grad_pre = (cot_ref[rows, :].astype(F32) * steep).astype(BF)
            spread = lax.dot_general(weight, grad_pre, (((1,), (1,)), ((), ())), preferred_element_type=F32)
            gpanel[col * B + t] = (spread * row_scale[t : t + 1, :]).astype(BF)
            outer = lax.dot_general(smoothed, grad_pre, (((0,), (0,)), ((), ())), preferred_element_type=F32)
            if t == 0:
                wlocal[...] = outer
            else:
                wlocal[...] += outer

    def grads_at(y, z, first=0, count=B):
        place = mod4(my + y) * 4 + masked(ml, z)
        return blocks(gpanel, place * B + first, count)

    def hand_on(dy, dz, first, count, **shift):
        ref = grads_at(dy, dz, first, count)
        return net.send(ref, ref, **shift)

    def back(half, y, z):
        first = (mod4(my + y) * 4 + masked(ml, z)) * B + 2 * half

        def tile(r):
            grads = gpanel[r]
            for k in range(0, K, 2):
                slot = r * K + k
                rhs = jnp.concatenate([entries[r, k], entries[r, k + 1]], axis=1)
                both = jnp.dot(grads, rhs, preferred_element_type=F32)
                one = chain[places[k, r]] + both[:, :T]
                two = chain[places[k + 1, r]] + both[:, T:]
                chain[slot] = one
                chain[slot + 1] = two

        for t in range(2):
            tile(first + t)

    gups, gdowns, fups, fdowns, gz = {}, {}, {}, {}, {}

    def along(h, mask):
        if mask > 0:
            gz[h, mask].wait_recv()
        gups[h, mask] = hand_on(0, mask, 2 * h, 2, y=1)
        gdowns[h, mask] = hand_on(0, mask, 2 * h, 2, y=3)

    def forward(h, mask):
        gups[h, mask].wait_recv()
        fups[h, mask] = hand_on(-1, mask, 2 * h, 1, y=1)
        gdowns[h, mask].wait_recv()
        fdowns[h, mask] = hand_on(1, mask, 2 * h + 1, 1, y=3)

    def over_z(h):
        for mask in (1, 2, 3):
            gz[h, mask] = hand_on(0, 0, 2 * h, 2, z=mask)

    def beside_back(h, mask):
        back(h, 3, mask)
        back(h, 1, mask)

    first(0, (0, 1))
    first(0, (2, 3))
    second(0, 0)
    second(0, 1)
    first(1, (0, 1))
    first(1, (2, 3))
    second(0, 2)
    second(0, 3)
    own(0)
    third(0, 0)
    second(1, 0)
    third(0, 1)
    second(1, 1)
    third(0, 2)
    second(1, 2)
    third(0, 3)
    second(1, 3)
    own(1)
    third(1, 0)
    net.drain(gathers)
    dense(0)
    along(0, 0)
    third(1, 1)
    third(1, 2)
    over_z(0)
    third(1, 3)
    back(0, 0, 0)
    forward(0, 0)
    along(0, 1)
    dense(1)
    along(1, 0)
    over_z(1)
    put_hidden = move(hidden_ref, hidden_hbm)
    wys = [
        net.send(wlocal.at[pl.ds(mod4(my + d) * 32, 32)], wy.at[d - 1], y=d) for d in (1, 2, 3)
    ]
    back(0, 0, 1)
    back(1, 0, 0)
    along(0, 2)
    along(0, 3)
    beside_back(0, 0)
    back(0, 0, 2)
    back(0, 0, 3)
    along(1, 1)
    forward(0, 1)
    forward(1, 0)
    back(1, 0, 1)
    beside_back(0, 1)
    beside_back(1, 0)
    along(1, 2)
    along(1, 3)
    for copy in wys:
        copy.wait_recv()
    wz[3] = wlocal[pl.ds(my * 32, 32), :] + wy[0] + wy[1] + wy[2]
    wzs = [
        net.send(wz.at[3, pl.ds(masked(ml, m) * 8, 8)], wz.at[m - 1, pl.ds(0, 8)], z=m) for m in (1, 2, 3)
    ]
    back(1, 0, 2)
    back(1, 0, 3)
    forward(0, 2)
    forward(0, 3)
    beside_back(0, 2)
    beside_back(0, 3)
    forward(1, 1)
    forward(1, 2)
    beside_back(1, 1)
    beside_back(1, 2)
    for copy in wzs:
        copy.wait_recv()
    wx[mx] = wz[3, pl.ds(ml * 8, 8), :] + wz[0, :8, :] + wz[1, :8, :] + wz[2, :8, :]
    wxs = [net.send(wx.at[mx], wx.at[mx], x=d) for d in (1, 2, 3)]
    forward(1, 3)
    beside_back(1, 3)
    for mask in range(4):
        fups[0, mask].wait_recv()
        fdowns[0, mask].wait_recv()
    for mask in range(4):
        back(0, 2, mask)
    for copy in wxs:
        copy.wait_recv()
    wc[0] = wx[0] + wx[1] + wx[2] + wx[3]
    wcs = net.send(wc.at[0], wc.at[1], core=1)
    for pair in ((0, 1), (2, 3)):
        for mask in pair:
            fups[1, mask].wait_recv()
            fdowns[1, mask].wait_recv()
        for mask in pair:
            back(1, 2, mask)
    wcs.wait_recv()
    wh[0] = wc[0] + wc[1]
    whs = net.send(wh.at[0], wh.at[1], half=1)

    def column(half, x, core):
        return (lax.rem(mz + half, 2) * 8 + mod4(mx + x) * 2 + lax.rem(mc + core, 2)) * B

    before_sums = len(net.made)
    order = [(half, x) for half in (1, 0) for x in (2, 1, 3, 0)]
    cores = []
    for n, (half, x) in enumerate(order):
        first = column(half, x, 1)
        for t in range(B):
            csend[n, t] = chain[places[LAST, first + t]].astype(BF)
        cores.append(net.send(csend.at[n], crecv.at[n], core=1))
    near, far = {}, {}

    def chip_sum(n):
        half, x = order[n]
        first = column(half, x, 0)
        cores[n].wait_recv()
        for t in range(B):
            xsum[n, t] = (chain[places[LAST, first + t]] + crecv[n, t].astype(F32)).astype(BF)

    def opposite(h, t):
        near[h, t] = (
            net.send(blocks(xsum.at[4 * h], t, 1), blocks(xup1.at[h], t // 2, 1), x=1),
            net.send(blocks(xsum.at[4 * h], t + 1, 1), blocks(xdown1.at[h], t // 2, 1), x=3),
        )

    def beside(h, t):
        up, down = near[h, t]
        up.wait_recv()
        right, left = xsum.at[4 * h + 1], xsum.at[4 * h + 2]
        right[t] = (right[t].astype(F32) + xup1[h, t // 2].astype(F32)).astype(BF)
        up = net.send(blocks(right, t, 2), blocks(xup2.at[h], t, 2), x=1)
        down.wait_recv()
        left[t + 1] = (left[t + 1].astype(F32) + xdown1[h, t // 2].astype(F32)).astype(BF)
        far[h, t] = (up, net.send(blocks(left, t, 2), blocks(xdown2.at[h], t, 2), x=3))

    def gathered(h, t):
        for copy in far[h, t]:
            copy.wait_recv()
        two = pl.ds(t, 2)
        return xsum[4 * h + 3, two].astype(F32) + xup2[h, two].astype(F32) + xdown2[h, two].astype(F32)

    across = []

    def cross(t):
        hsend[pl.ds(t, 2)] = gathered(0, t).astype(BF)
        across.append(net.send(blocks(hsend, t, 2), blocks(hrecv, t, 2), half=1))

    chip_sum(0)
    opposite(0, 0)
    opposite(0, 2)
    chip_sum(1)
    chip_sum(2)
    beside(0, 0)
    beside(0, 2)
    whs.wait_recv()
    wrows = my * 32 + ml * 8
    wfull[pl.ds(wrows, 8), :] = (wh[0] + wh[1]) * grad_scale
    wzs2 = [
        net.send(wfull.at[pl.ds(wrows, 8)], wfull.at[pl.ds(wrows, 8)], z=m) for m in (1, 2, 3)
    ]
    chip_sum(4)
    opposite(1, 0)
    opposite(1, 2)
    chip_sum(3)
    cross(0)
    cross(2)
    chip_sum(5)
    chip_sum(6)
    beside(1, 0)
    beside(1, 2)
    chip_sum(7)
    for copy in wzs2:
        copy.wait_recv()
    wband = wfull.at[pl.ds(my * 32, 32)]
    wys2 = [net.send(wband, wband, y=d) for d in (1, 2, 3)]
    net.drain(before_sums)
    puts = [put_hidden]
    for t, copy in zip(halves, across):
        here = gathered(1, t)
        copy.wait_recv()
        for u in range(2):
            tile = here[u] + hrecv[t + u].astype(F32)
            fgrad_ref[pl.ds((t + u) * T, T), :] = (tile * col_scale[t + u : t + u + 1, :]).T.astype(BF)
        part = pl.ds(t * T, 2 * T)
        puts.append(move(fgrad_ref.at[part], fgrad_hbm.at[part]))
    for copy in wys2:
        copy.wait_recv()
    puts.append(move(wfull, wgrad_hbm))
    net.drain(len(net.made))
    for put in puts:
        put.wait()


def find_places(cols_ref, mask_ref, found, my, ml):
    square = (TILES, TILES)

    def turn_of(r):
        dy = mod4(r // 16 - my)
        z = lax.rem(r // 4, 4)
        part = lax.rem(r // 2, 2)
        turn = jnp.zeros_like(r)
        for n, (half, y, mask) in enumerate(TURNS):
            turn = jnp.where((part == half) & (dy == y) & (z == masked(ml, mask)), n, turn)
        return turn * 2 + lax.rem(r, 2)

    over = lax.broadcasted_iota(jnp.int32, square, 1)
    down = lax.broadcasted_iota(jnp.int32, square, 0)
    turn_over = turn_of(over[:1])
    turn_down = turn_of(down)
    index = [jnp.where(mask_ref[k] > 0, cols_ref[k], ZERO) for k in range(K)]
    index_down = [jnp.broadcast_to(index[k], square).T for k in range(K)]
    key_down = [turn_down * 512 + down * K + k for k in range(K)]

    def slot_of(key, live):
        return jnp.where(live & (key >= 0), lax.rem(key, 512), EMPTY)

    ahead = turn_down < turn_over
    for k in range(K):
        best = jnp.full(square, -1, jnp.int32)
        for j in range(K):
            best = jnp.maximum(best, jnp.where(index_down[j] == index[k], key_down[j], -1))
        key = jnp.max(jnp.where(ahead, best, -1), axis=0, keepdims=True)
        found[k : k + 1, :TILES] = slot_of(key, index[k] < ZERO)
        found[INDEX + k : INDEX + k + 1, :TILES] = index[k]
    best = jnp.full(square, -1, jnp.int32)
    for j in range(K):
        best = jnp.maximum(best, jnp.where(index_down[j] == over, key_down[j], -1))
    key = jnp.max(best, axis=0, keepdims=True)
    found[LAST : LAST + 1, :TILES] = slot_of(key, key >= 0)


def finish(*refs):
    n = len(refs) // 2
    for source, target in zip(refs[:n], refs[n:]):
        target[...] = source[...]


def body(features, weight, row_degree, col_degree, tile_cols, slot_mask, tile_entries, cotangent):
    anywhere = pl.BlockSpec(memory_space=pl.ANY)
    vmem = pl.BlockSpec(memory_space=pltpu.VMEM)
    nodes, hidden_width = cotangent.shape
    count = nodes * lax.axis_size("row") * lax.axis_size("col")
    grad_scale = 1.0 / (32.0 * math.sqrt(count))

    def tiles(*lead, dtype=BF):
        return pltpu.VMEM((*lead, T, T), dtype)

    def wide(*shape):
        return pltpu.VMEM((*shape, hidden_width), F32)

    shapes = (
        jax.ShapeDtypeStruct((nodes, hidden_width), BF),
        jax.ShapeDtypeStruct((T, hidden_width), F32),
        jax.ShapeDtypeStruct((nodes, T), BF),
    )
    results = pl.pallas_call(
        functools.partial(kernel, grad_scale),
        out_shape=shapes,
        in_specs=[anywhere] * 8,
        out_specs=(anywhere,) * 3,
        scratch_shapes=[
            pltpu.VMEM((K, 1, TILES), jnp.int32), pltpu.VMEM((K, 1, TILES), jnp.int32),
            pltpu.VMEM((nodes, T), BF), pltpu.VMEM((T, hidden_width), BF),
            pltpu.VMEM((B, T), jnp.int32), pltpu.VMEM((B, T), jnp.int32),
            pltpu.VMEM((nodes, hidden_width), BF), pltpu.VMEM((nodes, hidden_width), BF), pltpu.VMEM((nodes, T), BF),
            pltpu.VMEM((16, 128), jnp.int32), pltpu.SMEM((16, 128), jnp.int32),
            tiles(TILES, K), tiles(TILES + 1), tiles(TILES),
            tiles(4, 2), tiles(4, 2), tiles(4, B), tiles(4, B), tiles(3, B), tiles(3, B), tiles(B, dtype=F32),
            tiles(TILES), tiles(SLOTS + 1, dtype=F32),
            wide(T), wide(3, 32), wide(4, 32), wide(4, 8), wide(2, 8), wide(2, 8), wide(T),
            tiles(8, B), tiles(8, B), tiles(8, B),
            tiles(2, 2), tiles(2, 2), tiles(2, B), tiles(2, B), tiles(B), tiles(B),
            pltpu.SemaphoreType.DMA((N_LOADS,)),
            pltpu.SemaphoreType.DMA((16,)),
            pltpu.SemaphoreType.DMA((N_COPIES,)),
            pltpu.SemaphoreType.DMA((N_COPIES,)),
        ],
        compiler_params=pltpu.CompilerParams(
            collective_id=0, has_side_effects=True, vmem_limit_bytes=60 * 1024 * 1024
        ),
        name="graph_layer",
    )(
        tile_cols.transpose(2, 1, 0), slot_mask.transpose(2, 1, 0), tile_entries.reshape(TILES, K, T, T),
        features, weight, row_degree.reshape(B, T), col_degree.reshape(B, T), cotangent,
    )
    return pl.pallas_call(
        finish,
        out_shape=shapes,
        in_specs=[vmem] * 3,
        out_specs=(vmem,) * 3,
        name="results",
    )(*results)


def solution(mesh):
    return jax.shard_map(
        body,
        mesh=mesh,
        in_specs=(
            P(("col", "row"), None),
            P(),
            P(("row", "col")),
            P(("col", "row")),
            P("row", "col", None),
            P("row", "col", None),
            P("row", "col", None, None, None),
            P(("row", "col"), None),
        ),
        out_specs=(P(("row", "col"), None), P(), P(("col", "row"), None)),
        check_vma=False,
    )
```
